256 devices in a mesh: blk: 32 (over z, y_lo, core), group: 8 (over y_hi, x).
Axes of the slice: x: 4, y: 4 (y_hi: 2, y_lo: 2; y = y_hi * 2 + y_lo), z: 8, core: 2. Of those that a mesh axis runs over, the one named last changes fastest.
Arguments:
- features: bfloat16 [8, 8192, 2048], P('group', 'blk'), may hold values from -0.29882812 to 0.29882812
- head_weight: bfloat16 [2048, 512], replicated, may hold values from -0.125 to 0.125
- pairs: int32 [8, 8192], P('group', 'blk'), may hold values from 0 to 8191, as said below
Outputs:
- pair_logit: float32 [8, 8192], P('group', 'blk')
- row_lse: float32 [8, 8192], P('group', 'blk')
- proj_grad: float32 [8, 8192, 512], P('group', 'blk')
- head_grad: float32 [2048, 512], replicated
The draws below stay inside these ranges and needn't reach their ends.
Inputs may be any that keep to these rules, and one draw needn't show every extreme that they name: pairs pairs each view with another view of the same group, and pairs[g, pairs[g, i]] = i.
All inputs are finite; a program needn't handle non-finite values.
Results may differ from the reference program's by a relative error of at most 0.004.
Values may be sent and summed in bfloat16 or wider, within the bound.
A program may use at most 64 MiB of HBM per device.

```python
import jax
import jax.numpy as jnp
from jax import lax

HID = 2048
PROJ = 512
GROUPS = 8
VIEWS = 8192


def pair_one(key):
    perm = jax.random.permutation(key, VIEWS)
    swapped = perm.reshape(-1, 2)[:, ::-1].reshape(-1)
    return jnp.zeros((VIEWS,), jnp.int32).at[perm].set(swapped.astype(jnp.int32))


def draw_pairs(key, part):
    key = jax.random.fold_in(key, 1)
    keys = jax.random.split(key, GROUPS)
    return jax.vmap(pair_one)(keys).astype(jnp.int32)


def levels(rng, extent, cuts, least, high):
    def one(dim, shards_of):
        steps = jax.random.uniform(jax.random.fold_in(jax.random.fold_in(rng, 6), dim), (shards_of,), jnp.float32, least / len(cuts), high / len(cuts))
        return jnp.repeat(jnp.exp(steps), extent[dim] // shards_of).reshape((-1,) + (1,) * (len(extent) - dim - 1))

    gain = one(*cuts[0])
    for cut in cuts[1:]:
        gain = gain * one(*cut)
    return gain


def gaussian(own_key, dims, spread, limit, cuts=(), kind=jnp.bfloat16):
    level = levels(own_key, dims, cuts, -0.22, 0.18) if cuts else 1.0
    result = jax.random.normal(own_key, dims, jnp.float32) * spread * level
    return jnp.minimum(jnp.maximum(result, -limit), limit).astype(kind)


def setup_inputs(seed: int = 0) -> dict:
    streams_of = jax.random.split(jax.random.key(seed), 4)
    features = gaussian(streams_of[0], (GROUPS, VIEWS, HID), 0.05, 0.29882812, ((0, 8), (1, 32)))
    head_weight = gaussian(streams_of[1], (HID, PROJ), HID ** -0.5, 0.125)
    pairs = draw_pairs(jax.random.fold_in(streams_of[3], 71), 0)
    return {"features": features, "head_weight": head_weight, "pairs": pairs}


logit_divisor = 0.1

def one_group(args, head_weight):
    feats, pairs = args
    z = jnp.dot(feats, head_weight, preferred_element_type=jnp.float32)
    inv = lax.rsqrt(lax.optimization_barrier(jnp.sum(z * z, axis=1)) + 1e-06)
    u = z * inv[:, None]
    sphere_embeddings = u.astype(jnp.bfloat16)
    cosine_affinity = jnp.dot(sphere_embeddings, sphere_embeddings.T, preferred_element_type=jnp.float32) / logit_divisor
    count = cosine_affinity.shape[0]
    idx = jnp.arange(count, dtype=jnp.int32)
    e = jnp.where(idx[:, None] == idx[None, :], jnp.zeros_like(cosine_affinity), jnp.exp(cosine_affinity))
    den = lax.optimization_barrier(jnp.sum(e, axis=1))
    lse = jnp.log(den)
    pairmask = pairs[:, None] == idx[None, :]
    pos = lax.optimization_barrier(jnp.sum(jnp.where(pairmask, cosine_affinity, jnp.zeros_like(cosine_affinity)), axis=1))
    linear_map_coefficients = e / den[:, None] + e / den[None, :] - 2.0 * pairmask.astype(cosine_affinity.dtype)
    rescaled_direction_slope = jnp.dot(linear_map_coefficients.astype(jnp.bfloat16), sphere_embeddings, preferred_element_type=jnp.float32) / logit_divisor
    dz = inv[:, None] * (rescaled_direction_slope - u * lax.optimization_barrier(jnp.sum(u * rescaled_direction_slope, axis=1, keepdims=True)))
    head_term = jnp.dot(feats.T, dz.astype(jnp.bfloat16), preferred_element_type=jnp.float32)
    return (pos, lse, dz, head_term)

def reference(features, head_weight, pairs):
    pos, lse, dz, terms = lax.map(lambda a: one_group(a, head_weight), (features, pairs))
    return (pos, lse, dz, lax.optimization_barrier(jnp.sum(terms, axis=0)))
```

```python
import functools

import jax
import jax.numpy as jnp
from jax import lax
from jax.experimental import pallas as pl
from jax.experimental.pallas import tpu as pltpu
from jax.sharding import PartitionSpec as P

MESH = pl.DeviceIdType.MESH
F32 = jnp.float32
BF16 = jnp.bfloat16

HID = 2048
PROJ = 512
ROWS = 256
NZ = 8
NA = 144
NB = ROWS - NA
INV_TEMP = 10.0
LOG2E = 1.4426950408889634

LAST = (
    ((0, 80), (80, 64)),
    ((NA, 48), (NA + 48, 64)),
    ((NA, 64), (NA + 64, 48)),
)


def kernel(
    feat_ref, w_ref, pairs_ref,
    pos_ref, lse_ref, dz_ref, head_ref,
    ub_all, e_all, u_s, inv_s, pcol_s, den_s, pos_s, rden_all, acc_s,
    f_sib, f_t, dzb, pf, sb1, r1, qf, r2, zb, r3, gz,
    z_send, z_recv, y_send, y_recv, c_send, c_recv, d_send, d_recv,
    x_send, x_recv, s1_send, s1_recv, s2_send, s2_recv, s3_send, s3_recv,
    g3_send, g3_recv, g2_send, g2_recv, g1_send, g1_recv, gc_send, gc_recv,
):
    blk = lax.axis_index("blk")
    grp = lax.axis_index("group")
    z, yl, c = blk // 4, lax.rem(blk // 2, 2), lax.rem(blk, 2)
    yh, x = grp // 4, lax.rem(grp, 4)
    y = yh * 2 + yl

    def dev(z_, y_, c_, x_):
        return ((z_ * 2 + lax.rem(y_, 2)) * 2 + c_, (y_ // 2) * 4 + x_)

    def copy(src, dst, ssem, rsem, to):
        return pltpu.make_async_remote_copy(
            src_ref=src, dst_ref=dst, send_sem=ssem, recv_sem=rsem,
            device_id=to, device_id_type=MESH,
        )

    sib = dev(z, y, 1 - c, x)
    ynb = (blk + 2 - 4 * yl, grp)

    barrier = pltpu.get_barrier_semaphore()

    def greet(i, carry):
        pl.semaphore_signal(
            barrier, inc=1, device_id=(lax.rem(blk + i, 32), grp), device_id_type=MESH
        )
        return carry

    lax.fori_loop(1, 32, greet, 0)
    for d in (1, 2, 3):
        pl.semaphore_signal(
            barrier, inc=1, device_id=dev(z, y, c, lax.rem(x + d, 4)), device_id_type=MESH
        )
    for yl_ in (0, 1):
        pl.semaphore_signal(
            barrier, inc=1, device_id=dev(z, (1 - yh) * 2 + yl_, c, x), device_id_type=MESH
        )

    zz = jnp.dot(feat_ref[...], w_ref[...], preferred_element_type=F32)
    inv = lax.rsqrt(jnp.sum(zz * zz, axis=1, keepdims=True) + 1e-06)
    u = zz * inv
    inv_s[...] = inv
    u_s[...] = u
    row0 = pl.multiple_of((yl * 2 + c) * ROWS, ROWS)
    ub_all[z, pl.ds(row0, ROWS), :] = u.astype(BF16)
    pl.semaphore_wait(barrier, 36)

    def origin(dr, s):
        return lax.rem(z + NZ + (-s if dr == 0 else s), NZ)

    def rows_of(yl_, c_, off, n):
        return pl.ds(pl.multiple_of((yl_ * 2 + c_) * ROWS + off, 16), n)

    def piece(zo, yl_, c_, off, n):
        return ub_all.at[zo, rows_of(yl_, c_, off, n), :]

    def z_copy(dr, s, kind):
        off, n = LAST[kind][dr] if s == 3 else ((0, NA) if kind == 0 else (NA, NB))
        ref = piece(origin(dr, s), 1 - yl if kind == 2 else yl, c, off, n)
        to = dev(lax.rem(z + (1 if dr == 0 else NZ - 1), NZ), y, c, x)
        return copy(ref, ref, z_send.at[dr, s, kind], z_recv.at[dr, s, kind], to)

    def z_arrived(dr, s, kind):
        off, n = LAST[kind][dr] if s == 3 else ((0, NA) if kind == 0 else (NA, NB))
        ref = piece(origin(dr, s + 1), 1 - yl if kind == 2 else yl, c, off, n)
        to = dev(lax.rem(z + (1 if dr == 0 else NZ - 1), NZ), y, c, x)
        return copy(ref, ref, z_send.at[dr, s, kind], z_recv.at[dr, s, kind], to)

    def y_ref(i, yl_):
        if i == 0:
            return piece(z, yl_, c, NA, NB)
        if i == 1:
            return piece(z, yl_, c, 0, NA)
        if i < 8:
            return piece(origin((i - 2) // 3, (i - 2) % 3 + 1), yl_, c, 0, NA)
        off, n = LAST[0][i - 8]
        return piece(origin(0, 4), yl_, c, off, n)

    def y_copy(i):
        ref = y_ref(i, yl)
        return copy(ref, ref, y_send.at[i], y_recv.at[i], ynb)

    def y_arrived(i):
        ref = y_ref(i, 1 - yl)
        return copy(ref, ref, y_send.at[i], y_recv.at[i], ynb)

    def c_ref(dr, s, other_y, c_):
        return piece(origin(dr, s), 1 - yl if other_y else yl, c_, 0, ROWS)

    def c_copy(dr, s, other_y):
        ref = c_ref(dr, s, other_y, c)
        i = (s * 2 + dr) * 2 + other_y
        return copy(ref, ref, c_send.at[i], c_recv.at[i], sib)

    def c_arrived(dr, s, other_y):
        ref = c_ref(dr, s, other_y, 1 - c)
        i = (s * 2 + dr) * 2 + other_y
        return copy(ref, ref, c_send.at[i], c_recv.at[i], sib)

    sent = []

    def go(cp):
        cp.start()
        sent.append(cp)

    go(y_copy(0))
    for dr in (0, 1):
        go(z_copy(dr, 0, 0))
    for dr in (0, 1):
        go(z_copy(dr, 0, 1))
    go(y_copy(1))
    go(c_copy(0, 0, 0))
    mine = pl.multiple_of(c * (HID // 2), HID // 2)
    theirs = pl.multiple_of((1 - c) * (HID // 2), HID // 2)
    xcp = copy(feat_ref.at[:, pl.ds(theirs, HID // 2)], f_sib, x_send.at[0], x_recv.at[0], sib)
    go(xcp)

    pcol_s[...] = jnp.broadcast_to(pairs_ref[...], (128, ROWS)).T[:, :1]
    den_s[...] = jnp.zeros_like(den_s)
    pos_s[...] = jnp.zeros_like(pos_s)
    own_row = blk * ROWS + lax.broadcasted_iota(jnp.int32, (ROWS, 1), 0)

    def scores(zo, j):
        block = ub_all[zo, pl.ds(pl.multiple_of(j * ROWS, ROWS), ROWS), :]
        mine_ub = ub_all[z, pl.ds(row0, ROWS), :]
        s = lax.dot_general(
            mine_ub, block, (((1,), (1,)), ((), ())), preferred_element_type=F32
        )
        cols = (zo * 4 + j) * ROWS + lax.broadcasted_iota(jnp.int32, (ROWS, ROWS), 1)
        e = jnp.where(cols == own_row, 0.0, jnp.exp2(s * (INV_TEMP * LOG2E)))
        e_all[zo, :, pl.ds(pl.multiple_of(j * ROWS, ROWS), ROWS)] = e
        p = jnp.where(cols == pcol_s[...], s, 0.0)
        den_s[...] += e[:, :128] + e[:, 128:]
        pos_s[...] += p[:, :128] + p[:, 128:]

    def scores_of(zo):
        def body(j, carry):
            scores(zo, j)
            return carry

        lax.fori_loop(0, 4, body, 0)

    y_arrived(0).wait_recv()
    for dr in (0, 1):
        go(z_copy(dr, 0, 2))
    f_t[:, :ROWS] = feat_ref[:, pl.ds(mine, HID // 2)].T
    y_arrived(1).wait_recv()
    go(c_copy(0, 0, 1))
    xcp.wait_recv()
    f_t[:, ROWS:] = f_sib[...].T

    for s in (1, 2, 3, 4):
        drs = (0, 1)
        for kind in (0, 1, 2):
            for dr in drs:
                z_arrived(dr, s - 1, kind).wait_recv()
                if s < 4:
                    go(z_copy(dr, s, kind))
                if kind == 0:
                    go(y_copy(2 + dr * 3 + s - 1) if s < 4 else y_copy(8 + dr))
            if kind == 1:
                for dr in drs if s < 4 else (0,):
                    go(c_copy(dr, s, 0))
        for dr in drs if s > 1 else (0,):
            for oy in (0, 1):
                c_arrived(dr, s - 1, oy).wait_recv()
            scores_of(origin(dr, s - 1))
        for dr in drs:
            y_arrived(2 + dr * 3 + s - 1 if s < 4 else 8 + dr).wait_recv()
            if s < 4 or dr == 1:
                go(c_copy(dr if s < 4 else 0, s, 1))
    for oy in (0, 1):
        c_arrived(0, 4, oy).wait_recv()
    scores_of(origin(0, 4))

    den = jnp.sum(den_s[...], axis=1, keepdims=True)
    r_own = 1.0 / den
    rden_all[blk] = jnp.broadcast_to(r_own, (ROWS, 128)).T[:1, :]

    def d_copy(dz_, k):
        to_blk = lax.rem(z + dz_, NZ) * 4 + lax.rem(yl + k // 2, 2) * 2 + lax.rem(c + k % 2, 2)
        i = dz_ * 4 + k
        return copy(
            rden_all.at[blk], rden_all.at[blk], d_send.at[i], d_recv.at[i], (to_blk, grp)
        )

    def d_arrived(dz_, k):
        i = dz_ * 4 + k
        from_blk = (
            lax.rem(z + NZ - dz_, NZ) * 4
            + lax.rem(yl + k // 2, 2) * 2
            + lax.rem(c + k % 2, 2)
        )
        ref = rden_all.at[from_blk]
        return copy(ref, ref, d_send.at[i], d_recv.at[i], (blk, grp))

    for dz_ in (4, 3, 5, 2, 6, 1, 7, 0):
        for k in range(4):
            if dz_ or k:
                go(d_copy(dz_, k))

    lse_ref[...] = jnp.broadcast_to(jnp.log(den), (ROWS, 128)).T[:1, :]
    pos = jnp.sum(pos_s[...], axis=1, keepdims=True) * INV_TEMP
    pos_ref[...] = jnp.broadcast_to(pos, (ROWS, 128)).T[:1, :]

    for n, dz_ in enumerate((0, 1, 7, 2, 6, 3, 5, 4)):
        for k in range(4):
            if dz_ or k:
                d_arrived(dz_, k).wait_recv()
        zo = lax.rem(z + NZ - dz_, NZ)
        parts = []
        for j in range(4):
            cols = (zo * 4 + j) * ROWS + lax.broadcasted_iota(jnp.int32, (ROWS, ROWS), 1)
            e = e_all[zo, :, j * ROWS : (j + 1) * ROWS]
            h = e * (r_own + rden_all[zo * 4 + j]) - jnp.where(cols == pcol_s[...], 2.0, 0.0)
            parts.append(h.astype(BF16))
        g = jnp.dot(
            jnp.concatenate(parts, axis=1), ub_all[zo], preferred_element_type=F32
        )
        if n == 0:
            acc_s[...] = g
        else:
            acc_s[...] += g

    slope = acc_s[...] * INV_TEMP
    u = u_s[...]
    dz = inv_s[...] * (slope - u * jnp.sum(u * slope, axis=1, keepdims=True))
    dz_ref[...] = dz
    dzb[0] = dz.astype(BF16)
    xcp = copy(dzb.at[0], dzb.at[1], x_send.at[1], x_recv.at[1], sib)
    go(xcp)
    xcp.wait_recv()

    def along(t, first, d):
        if (t % 2 == 0) == first:
            return dev(z, y, c, lax.rem(x + d, 4))
        return dev(z, lax.rem(y + d, 4), c, x)

    def place(t, first):
        return x if (t % 2 == 0) == first else y

    def s1_copy(t, d):
        j = lax.rem(place(t, True) + d, 4)
        return copy(sb1.at[t, j], r1.at[t, d - 1], s1_send.at[t, d - 1], s1_recv.at[t, d - 1], along(t, True, d))

    def s2_copy(t, d):
        j = lax.rem(place(t, False) + d, 4)
        return copy(qf.at[t, j], r2.at[t, d - 1], s2_send.at[t, d - 1], s2_recv.at[t, d - 1], along(t, False, d))

    def zslice(ref, p, j):
        return ref.at[p, :, pl.ds(pl.multiple_of((j // 4) * 8, 8), 8), pl.ds(pl.multiple_of(lax.rem(j, 4) * 128, 128), 128)]

    def zpeer(d):
        return dev(lax.rem(z + d, NZ), y, c, x)

    def s3_copy(p, d):
        j = lax.rem(z + d, NZ)
        return copy(zslice(zb, p, j), r3.at[p, d - 1], s3_send.at[p, d - 1], s3_recv.at[p, d - 1], zpeer(d))

    def g3_copy(p, d, mine_=True):
        ref = zslice(gz, p, z if mine_ else lax.rem(z + NZ - d, NZ))
        return copy(ref, ref, g3_send.at[p, d - 1], g3_recv.at[p, d - 1], zpeer(d))

    def out_rows(t, a, b, n):
        start = c * (HID // 2) + t * 256 + a * 64 + b * 16
        return head_ref.at[pl.ds(pl.multiple_of(start, 16), n), :]

    def g2_copy(t, d, mine_=True):
        b = place(t, False)
        ref = out_rows(t, place(t, True), b if mine_ else lax.rem(b + 4 - d, 4), 16)
        return copy(ref, ref, g2_send.at[t, d - 1], g2_recv.at[t, d - 1], along(t, False, d))

    def g1_copy(t, d, mine_=True):
        a = place(t, True)
        ref = out_rows(t, a if mine_ else lax.rem(a + 4 - d, 4), 0, 64)
        return copy(ref, ref, g1_send.at[t, d - 1], g1_recv.at[t, d - 1], along(t, True, d))

    def gc_copy(t, d):
        a = place(t, True)
        ref = out_rows(t, lax.rem(a + 4 - d, 4), 0, 64)
        return copy(ref, ref, gc_send.at[t, d], gc_recv.at[t, d], sib)

    def gc_arrived(t, d):
        start = (1 - c) * (HID // 2) + t * 256 + lax.rem(place(t, True) + 4 - d, 4) * 64
        ref = head_ref.at[pl.ds(pl.multiple_of(start, 64), 64), :]
        return copy(ref, ref, gc_send.at[t, d], gc_recv.at[t, d], sib)

    D3, D7 = (2, 1, 3), (4, 3, 5, 2, 6, 1, 7)

    def stage1(t):
        dzs = jnp.concatenate([dzb[0], dzb[1]], axis=0)
        part = jnp.dot(f_t[t * 256 : (t + 1) * 256, :], dzs, preferred_element_type=F32)
        pf[t] = part.reshape(4, 64, PROJ)
        sb1[t] = part.astype(BF16).reshape(4, 64, PROJ)
        for d in D3:
            go(s1_copy(t, d))

    def stage2(t):
        for d in D3:
            s1_copy(t, d).wait_recv()
        total = pf[t, place(t, True)]
        for d in range(3):
            total = total + r1[t, d].astype(F32)
        qf[t] = total.reshape(4, 16, PROJ)
        for d in D3:
            go(s2_copy(t, d))

    def stage3(p):
        for i in (0, 1):
            t = 2 * p + i
            for d in D3:
                s2_copy(t, d).wait_recv()
            zb[p, i] = qf[t, place(t, False)] + r2[t, 0] + r2[t, 1] + r2[t, 2]
        for d in D7:
            go(s3_copy(p, d))

    def stage4(p):
        for d in D7:
            s3_copy(p, d).wait_recv()
        rows = pl.ds(pl.multiple_of((z // 4) * 8, 8), 8)
        cols = pl.ds(pl.multiple_of(lax.rem(z, 4) * 128, 128), 128)
        total = zb[p, :, rows, cols]
        for d in range(7):
            total = total + r3[p, d]
        gz[p, :, rows, cols] = total
        for d in D7:
            go(g3_copy(p, d))

    def stage5(p):
        for d in D7:
            g3_copy(p, d, False).wait_recv()
        for i in (0, 1):
            t = 2 * p + i
            start = c * (HID // 2) + t * 256 + place(t, True) * 64 + place(t, False) * 16
            head_ref[pl.ds(pl.multiple_of(start, 16), 16), :] = gz[p, i].astype(BF16)
            for d in D3:
                go(g2_copy(t, d))

    def stage6(t):
        for d in D3:
            g2_copy(t, d, False).wait_recv()
        for d in D3:
            go(g1_copy(t, d))
        go(gc_copy(t, 0))

    def stage7(t):
        for d in D3:
            g1_copy(t, d, False).wait_recv()
            go(gc_copy(t, d))

    for t in range(4):
        stage1(t)
    stage2(0)
    stage2(1)
    stage3(0)
    stage2(2)
    stage2(3)
    stage4(0)
    stage3(1)
    stage5(0)
    stage4(1)
    stage6(0)
    stage6(1)
    stage5(1)
    stage6(2)
    stage6(3)
    for t in range(4):
        stage7(t)
    for t in range(4):
        for d in range(4):
            gc_arrived(t, d).wait_recv()
    for cp in sent:
        cp.wait_send()


def on_device(features, head_weight, pairs):
    vmem = pl.BlockSpec(memory_space=pltpu.VMEM)
    dma = pltpu.SemaphoreType.DMA
    pos, lse, dz, head = pl.pallas_call(
        kernel,
        out_shape=(
            jax.ShapeDtypeStruct((1, ROWS), F32),
            jax.ShapeDtypeStruct((1, ROWS), F32),
            jax.ShapeDtypeStruct((ROWS, PROJ), F32),
            jax.ShapeDtypeStruct((HID, PROJ), BF16),
        ),
        in_specs=[vmem] * 3,
        out_specs=(vmem,) * 4,
        scratch_shapes=[
            pltpu.VMEM((NZ, 4 * ROWS, PROJ), BF16),
            pltpu.VMEM((NZ, ROWS, 4 * ROWS), F32),
            pltpu.VMEM((ROWS, PROJ), F32),
            pltpu.VMEM((ROWS, 1), F32),
            pltpu.VMEM((ROWS, 1), jnp.int32),
            pltpu.VMEM((ROWS, 128), F32),
            pltpu.VMEM((ROWS, 128), F32),
            pltpu.VMEM((32, 1, ROWS), F32),
            pltpu.VMEM((ROWS, PROJ), F32),
            pltpu.VMEM((ROWS, HID // 2), BF16),
            pltpu.VMEM((HID // 2, 2 * ROWS), BF16),
            pltpu.VMEM((2, ROWS, PROJ), BF16),
            pltpu.VMEM((4, 4, 64, PROJ), F32),
            pltpu.VMEM((4, 4, 64, PROJ), BF16),
            pltpu.VMEM((4, 3, 64, PROJ), BF16),
            pltpu.VMEM((4, 4, 16, PROJ), F32),
            pltpu.VMEM((4, 3, 16, PROJ), F32),
            pltpu.VMEM((2, 2, 16, PROJ), F32),
            pltpu.VMEM((2, 7, 2, 8, 128), F32),
            pltpu.VMEM((2, 2, 16, PROJ), F32),
            dma((2, 4, 3)), dma((2, 4, 3)),
            dma((10,)), dma((10,)),
            dma((20,)), dma((20,)),
            dma((32,)), dma((32,)),
            dma((2,)), dma((2,)),
            dma((4, 3)), dma((4, 3)),
            dma((4, 3)), dma((4, 3)),
            dma((2, 7)), dma((2, 7)),
            dma((2, 7)), dma((2, 7)),
            dma((4, 3)), dma((4, 3)),
            dma((4, 3)), dma((4, 3)),
            dma((4, 4)), dma((4, 4)),
        ],
        compiler_params=pltpu.CompilerParams(
            collective_id=0, has_side_effects=True, vmem_limit_bytes=60 << 20
        ),
        name="ntxent",
    )(features[0], head_weight, pairs)
    return pos, lse, dz[None], head.astype(F32)


def solution(mesh):
    in_specs = (P("group", "blk", None), P(), P("group", "blk"))
    out_specs = (P("group", "blk"), P("group", "blk"), P("group", "blk", None), P())
    return jax.shard_map(
        on_device, mesh=mesh, in_specs=in_specs, out_specs=out_specs, check_vma=False
    )
```

```python
import functools

import jax
import jax.numpy as jnp
from jax import lax
from jax.experimental import pallas as pl
from jax.experimental.pallas import tpu as pltpu
from jax.sharding import PartitionSpec as P

MESH = pl.DeviceIdType.MESH
F32 = jnp.float32
BF16 = jnp.bfloat16

HID = 2048
PROJ = 512
ROWS = 256
NZ = 8
NA = (176, 160)
INV_TEMP = 10.0
LOG2E = 1.4426950408889634

LAST = (((0, 144), (144, 112)), ((128, 128), (0, 128)))


def kernel(
    feat_ref, w_ref, pairs_ref,
    pos_ref, lse_ref, dz_ref, head_ref,
    ub_all, e_all, u_s, inv_s, pcol_s, den_s, pos_s, rden_all, acc_s,
    f_sib, f_t, dzb, pf, sb1, r1, qf, r2, zb, r3, in_sem,
    z_send, z_recv, y_send, y_recv, c_send, c_recv, d_send, d_recv,
    x_send, x_recv, s1_send, s1_recv, s2_send, s2_recv, s3_send, s3_recv,
    g3_send, g3_recv, g2_send, g2_recv, g1_send, g1_recv, gc_send, gc_recv,
):
    blk = lax.axis_index("blk")
    grp = lax.axis_index("group")
    z, yl, c = blk // 4, lax.rem(blk // 2, 2), lax.rem(blk, 2)
    yh, x = grp // 4, lax.rem(grp, 4)
    y = yh * 2 + yl

    def dev(z_, y_, c_, x_):
        return ((z_ * 2 + lax.rem(y_, 2)) * 2 + c_, (y_ // 2) * 4 + x_)

    def copy(src, dst, ssem, rsem, to):
        return pltpu.make_async_remote_copy(
            src_ref=src, dst_ref=dst, send_sem=ssem, recv_sem=rsem,
            device_id=to, device_id_type=MESH,
        )

    sib = dev(z, y, 1 - c, x)
    ynb = (blk + 2 - 4 * yl, grp)

    barrier = pltpu.get_barrier_semaphore()
    ring = (
        dev(z, y, c, lax.rem(x + 1, 4)),
        dev(z, y, c, lax.rem(x + 3, 4)),
        dev(z, lax.rem(y + 1, 4), c, x),
        dev(z, lax.rem(y + 3, 4), c, x),
    )
    znext = (dev(lax.rem(z + 1, NZ), y, c, x), dev(lax.rem(z + NZ - 1, NZ), y, c, x))
    for to in znext + (sib,) + ring:
        pl.semaphore_signal(barrier, inc=1, device_id=to, device_id_type=MESH)

    zz = jnp.dot(feat_ref[...], w_ref[...], preferred_element_type=F32)
    inv = lax.rsqrt(jnp.sum(zz * zz, axis=1, keepdims=True) + 1e-06)
    u = zz * inv
    inv_s[...] = inv
    u_s[...] = u
    row0 = pl.multiple_of((yl * 2 + c) * ROWS, ROWS)
    ub_all[z, pl.ds(row0, ROWS), :] = u.astype(BF16)
    pl.semaphore_wait(barrier, 7)

    def origin(dr, s):
        return lax.rem(z + NZ + (-s if dr == 0 else s), NZ)

    def rows_of(yl_, c_, off, n):
        return pl.ds(pl.multiple_of((yl_ * 2 + c_) * ROWS + off, 16), n)

    def piece(zo, yl_, c_, off, n):
        return ub_all.at[zo, rows_of(yl_, c_, off, n), :]

    def z_ref(dr, s, kind, zo):
        if s == 3:
            return piece(zo, 1 - yl if kind else yl, c, *LAST[kind][dr])
        na = NA[dr]
        return piece(zo, 1 - yl if kind == 2 else yl, c, *((na, ROWS - na) if kind else (0, na)))

    def z_copy(dr, s, kind):
        ref = z_ref(dr, s, kind, origin(dr, s))
        return copy(ref, ref, z_send.at[dr, s, kind], z_recv.at[dr, s, kind], znext[dr])

    def z_arrived(dr, s, kind):
        ref = z_ref(dr, s, kind, origin(dr, s + 1))
        return copy(ref, ref, z_send.at[dr, s, kind], z_recv.at[dr, s, kind], znext[dr])

    def y_ref(dr, s, yl_):
        if s == 0:
            return piece(z, yl_, c, *((NA[1], ROWS - NA[1]) if dr == 0 else (0, NA[1])))
        return piece(origin(dr, s), yl_, c, 0, NA[dr])

    def y_copy(dr, s):
        ref = y_ref(dr, s, yl)
        return copy(ref, ref, y_send.at[dr, s], y_recv.at[dr, s], ynb)

    def y_arrived(dr, s):
        ref = y_ref(dr, s, 1 - yl)
        return copy(ref, ref, y_send.at[dr, s], y_recv.at[dr, s], ynb)

    def c_ref(dr, s, other, c_):
        part = LAST[other][dr] if s == 4 else (0, ROWS)
        return piece(origin(dr, s), 1 - yl if other else yl, c_, *part)

    def c_copy(dr, s, other):
        ref = c_ref(dr, s, other, c)
        return copy(ref, ref, c_send.at[dr, s, other], c_recv.at[dr, s, other], sib)

    def c_arrived(dr, s, other):
        ref = c_ref(dr, s, other, 1 - c)
        return copy(ref, ref, c_send.at[dr, s, other], c_recv.at[dr, s, other], sib)

    sent = []

    def go(cp):
        cp.start()
        sent.append(cp)

    def flush():
        for cp in sent:
            cp.wait_send()
        sent.clear()

    go(y_copy(0, 0))
    for kind in (0, 1):
        for dr in (0, 1):
            go(z_copy(dr, 0, kind))
    go(y_copy(1, 0))
    go(c_copy(0, 0, 0))
    for to in ring:
        pl.semaphore_signal(in_sem, inc=1, device_id=to, device_id_type=MESH)
    mine = pl.multiple_of(c * (HID // 2), HID // 2)
    theirs = pl.multiple_of((1 - c) * (HID // 2), HID // 2)
    xcp = copy(feat_ref.at[:, pl.ds(theirs, HID // 2)], f_sib, x_send.at[0], x_recv.at[0], sib)
    go(xcp)

    pcol_s[...] = jnp.broadcast_to(pairs_ref[...], (128, ROWS)).T[:, :1]
    den_s[...] = jnp.zeros_like(den_s)
    pos_s[...] = jnp.zeros_like(pos_s)
    own_row = blk * ROWS + lax.broadcasted_iota(jnp.int32, (ROWS, 1), 0)

    def scores(zo, j):
        block = ub_all[zo, pl.ds(pl.multiple_of(j * ROWS, ROWS), ROWS), :]
        mine_ub = ub_all[z, pl.ds(row0, ROWS), :]
        s = lax.dot_general(
            mine_ub, block, (((1,), (1,)), ((), ())), preferred_element_type=F32
        )
        cols = (zo * 4 + j) * ROWS + lax.broadcasted_iota(jnp.int32, (ROWS, ROWS), 1)
        e = jnp.where(cols == own_row, 0.0, jnp.exp2(s * (INV_TEMP * LOG2E)))
        e_all[zo, :, pl.ds(pl.multiple_of(j * ROWS, ROWS), ROWS)] = e
        p = jnp.where(cols == pcol_s[...], s, 0.0)
        den_s[...] += e[:, :128] + e[:, 128:]
        pos_s[...] += p[:, :128] + p[:, 128:]

    def scores_of(zo):
        def body(j, carry):
            scores(zo, j)
            return carry

        lax.fori_loop(0, 4, body, 0)

    y_arrived(0, 0).wait_recv()
    for dr in (0, 1):
        go(z_copy(dr, 0, 2))
    f_t[:, :ROWS] = feat_ref[:, pl.ds(mine, HID // 2)].T
    y_arrived(1, 0).wait_recv()
    go(c_copy(0, 0, 1))
    xcp.wait_recv()
    f_t[:, ROWS:] = f_sib[...].T

    for s in (1, 2, 3):
        last = s == 3
        for dr in (0, 1):
            z_arrived(dr, s - 1, 0).wait_recv()
            if not last:
                go(z_copy(dr, s, 0))
            elif dr == 0:
                go(z_copy(0, 3, 0))
            go(y_copy(dr, s))
        for dr in (0, 1):
            z_arrived(dr, s - 1, 1).wait_recv()
            if not last:
                go(z_copy(dr, s, 1))
            elif dr == 1:
                go(z_copy(1, 3, 0))
            go(c_copy(dr, s, 0))
        for dr in (0, 1):
            z_arrived(dr, s - 1, 2).wait_recv()
            if not last:
                go(z_copy(dr, s, 2))
        for dr in (0, 1) if s > 1 else (0,):
            for other in (0, 1):
                c_arrived(dr, s - 1, other).wait_recv()
            scores_of(origin(dr, s - 1))
        for dr in (0, 1):
            y_arrived(dr, s).wait_recv()
            if last:
                go(z_copy(dr, 3, 1))
            go(c_copy(dr, s, 1))
    for dr in (0, 1):
        for other in (0, 1):
            c_arrived(dr, 3, other).wait_recv()
        scores_of(origin(dr, 3))
    flush()
    pl.semaphore_wait(in_sem, 4)
    far = origin(0, 4)
    for other in (0, 1):
        for dr in (0, 1):
            z_arrived(dr, 3, other).wait_recv()
            go(c_copy(dr, 4, other))
        scores(far, (1 - yl if other else yl) * 2 + c)
    for other in (0, 1):
        for dr in (0, 1):
            c_arrived(dr, 4, other).wait_recv()
        scores(far, (1 - yl if other else yl) * 2 + 1 - c)

    den = jnp.sum(den_s[...], axis=1, keepdims=True)
    r_own = 1.0 / den
    rden_all[blk] = jnp.broadcast_to(r_own, (ROWS, 128)).T[:1, :]

    def d_copy(dz_, k):
        to_blk = lax.rem(z + dz_, NZ) * 4 + lax.rem(yl + k // 2, 2) * 2 + lax.rem(c + k % 2, 2)
        i = dz_ * 4 + k
        return copy(
            rden_all.at[blk], rden_all.at[blk], d_send.at[i], d_recv.at[i], (to_blk, grp)
        )

    def d_arrived(dz_, k):
        i = dz_ * 4 + k
        from_blk = (
            lax.rem(z + NZ - dz_, NZ) * 4
            + lax.rem(yl + k // 2, 2) * 2
            + lax.rem(c + k % 2, 2)
        )
        ref = rden_all.at[from_blk]
        return copy(ref, ref, d_send.at[i], d_recv.at[i], (blk, grp))

    for dz_ in (4, 3, 5, 2, 6, 1, 7, 0):
        for k in range(4):
            if dz_ or k:
                go(d_copy(dz_, k))

    lse_ref[...] = jnp.broadcast_to(jnp.log(den), (ROWS, 128)).T[:1, :]
    pos = jnp.sum(pos_s[...], axis=1, keepdims=True) * INV_TEMP
    pos_ref[...] = jnp.broadcast_to(pos, (ROWS, 128)).T[:1, :]

    for n, dz_ in enumerate((0, 1, 7, 2, 6, 3, 5, 4)):
        for k in range(4):
            if dz_ or k:
                d_arrived(dz_, k).wait_recv()
        zo = lax.rem(z + NZ - dz_, NZ)
        parts = []
        for j in range(4):
            cols = (zo * 4 + j) * ROWS + lax.broadcasted_iota(jnp.int32, (ROWS, ROWS), 1)
            e = e_all[zo, :, j * ROWS : (j + 1) * ROWS]
            h = e * (r_own + rden_all[zo * 4 + j]) - jnp.where(cols == pcol_s[...], 2.0, 0.0)
            parts.append(h.astype(BF16))
        g = jnp.dot(
            jnp.concatenate(parts, axis=1), ub_all[zo], preferred_element_type=F32
        )
        if n == 0:
            acc_s[...] = g
        else:
            acc_s[...] += g

    slope = acc_s[...] * INV_TEMP
    u = u_s[...]
    dz = inv_s[...] * (slope - u * jnp.sum(u * slope, axis=1, keepdims=True))
    dz_ref[...] = dz
    dzb[0] = dz.astype(BF16)
    xcp = copy(dzb.at[0], dzb.at[1], x_send.at[1], x_recv.at[1], sib)
    go(xcp)
    xcp.wait_recv()

    def along(t, first, d):
        if (t % 2 == 0) == first:
            return dev(z, y, c, lax.rem(x + d, 4))
        return dev(z, lax.rem(y + d, 4), c, x)

    def place(t, first):
        return x if (t % 2 == 0) == first else y

    def s1_copy(t, d):
        j = lax.rem(place(t, True) + d, 4)
        return copy(sb1.at[t, j], r1.at[t, d - 1], s1_send.at[t, d - 1], s1_recv.at[t, d - 1], along(t, True, d))

    def s2_copy(t, d):
        j = lax.rem(place(t, False) + d, 4)
        return copy(qf.at[t, j], r2.at[t, d - 1], s2_send.at[t, d - 1], s2_recv.at[t, d - 1], along(t, False, d))

    def out_rows(t, a, b, n):
        start = c * (HID // 2) + t * 256 + a * 64 + b * 16
        return pl.ds(pl.multiple_of(start, 16), n)

    def zcols(j):
        return pl.ds(pl.multiple_of(lax.rem(j, 2) * 256, 256), 256)

    def zpeer(d):
        return dev(lax.rem(z + d, NZ), y, c, x)

    def s3_copy(d):
        j = lax.rem(z + d, NZ)
        return copy(zb.at[j // 2, :, zcols(j)], r3.at[d - 1], s3_send.at[d - 1], s3_recv.at[d - 1], zpeer(d))

    def zrows(j):
        t = j // 2
        odd = lax.rem(t, 2)
        return out_rows(t, x + odd * (y - x), y + odd * (x - y), 16)

    def g3_copy(d, mine_=True):
        j = z if mine_ else lax.rem(z + NZ - d, NZ)
        ref = head_ref.at[zrows(j), zcols(j)]
        return copy(ref, ref, g3_send.at[d - 1], g3_recv.at[d - 1], zpeer(d))

    def g2_copy(t, d, mine_=True):
        b = place(t, False)
        ref = head_ref.at[out_rows(t, place(t, True), b if mine_ else lax.rem(b + 4 - d, 4), 16), :]
        return copy(ref, ref, g2_send.at[t, d - 1], g2_recv.at[t, d - 1], along(t, False, d))

    def g1_copy(t, d, mine_=True):
        a = place(t, True)
        ref = head_ref.at[out_rows(t, a if mine_ else lax.rem(a + 4 - d, 4), 0, 64), :]
        return copy(ref, ref, g1_send.at[t, d - 1], g1_recv.at[t, d - 1], along(t, True, d))

    def gc_copy(t, d):
        a = place(t, True)
        ref = head_ref.at[out_rows(t, lax.rem(a + 4 - d, 4), 0, 64), :]
        return copy(ref, ref, gc_send.at[t, d], gc_recv.at[t, d], sib)

    def gc_arrived(t, d):
        start = (1 - c) * (HID // 2) + t * 256 + lax.rem(place(t, True) + 4 - d, 4) * 64
        ref = head_ref.at[pl.ds(pl.multiple_of(start, 64), 64), :]
        return copy(ref, ref, gc_send.at[t, d], gc_recv.at[t, d], sib)

    D3, D7 = (2, 1, 3), (4, 3, 5, 2, 6, 1, 7)

    def stage1(t):
        dzs = jnp.concatenate([dzb[0], dzb[1]], axis=0)
        part = jnp.dot(f_t[t * 256 : (t + 1) * 256, :], dzs, preferred_element_type=F32)
        pf[t] = part.reshape(4, 64, PROJ)
        sb1[t] = part.astype(BF16).reshape(4, 64, PROJ)
        for d in D3:
            go(s1_copy(t, d))

    def stage2(t):
        for d in D3:
            s1_copy(t, d).wait_recv()
        total = pf[t, place(t, True)]
        for d in range(3):
            total = total + r1[t, d].astype(F32)
        qf[t] = total.reshape(4, 16, PROJ)
        for d in D3:
            go(s2_copy(t, d))

    def stage3():
        for t in range(4):
            for d in D3:
                s2_copy(t, d).wait_recv()
            zb[t] = qf[t, place(t, False)] + r2[t, 0] + r2[t, 1] + r2[t, 2]
        for d in D7:
            go(s3_copy(d))

    def stage4():
        total = zb[z // 2, :, zcols(z)]
        for d in D7:
            s3_copy(d).wait_recv()
        for d in range(7):
            total = total + r3[d]
        head_ref[zrows(z), zcols(z)] = total.astype(BF16)
        for d in D7:
            go(g3_copy(d))

    def stage5():
        for d in D7:
            g3_copy(d, False).wait_recv()
        for t in range(4):
            for d in D3:
                go(g2_copy(t, d))

    def stage6(t):
        for d in D3:
            g2_copy(t, d, False).wait_recv()
        for d in D3:
            go(g1_copy(t, d))
        go(gc_copy(t, 0))

    def stage7(t):
        for d in D3:
            g1_copy(t, d, False).wait_recv()
            go(gc_copy(t, d))

    for t in range(4):
        stage1(t)
    for t in range(4):
        stage2(t)
    stage3()
    flush()
    stage4()
    stage5()
    flush()
    for t in range(4):
        stage6(t)
    for t in range(4):
        stage7(t)
    for t in range(4):
        for d in range(4):
            gc_arrived(t, d).wait_recv()
    flush()


def finish(pos_in, lse_in, dz_in, head_in, pos_ref, lse_ref, dz_ref, head_ref, buf, sem):
    copies = [
        pltpu.make_async_copy(dz_in, dz_ref, sem.at[0]),
        pltpu.make_async_copy(pos_in, pos_ref, sem.at[1]),
        pltpu.make_async_copy(lse_in, lse_ref, sem.at[2]),
    ]
    for cp in copies:
        cp.start()
    for i in range(8):
        rows = slice(i * 256, (i + 1) * 256)
        buf[rows, :] = head_in[rows, :].astype(F32)
        cp = pltpu.make_async_copy(buf.at[rows, :], head_ref.at[rows, :], sem.at[3 + i])
        cp.start()
        copies.append(cp)
    for cp in copies:
        cp.wait()


def on_device(features, head_weight, pairs):
    vmem = pl.BlockSpec(memory_space=pltpu.VMEM)
    dma = pltpu.SemaphoreType.DMA
    pos, lse, dz, head = pl.pallas_call(
        kernel,
        out_shape=(
            pltpu.VMEM((1, ROWS), F32),
            pltpu.VMEM((1, ROWS), F32),
            pltpu.VMEM((ROWS, PROJ), F32),
            pltpu.VMEM((HID, PROJ), BF16),
        ),
        in_specs=[vmem] * 3,
        out_specs=(vmem,) * 4,
        scratch_shapes=[
            pltpu.VMEM((NZ, 4 * ROWS, PROJ), BF16),
            pltpu.VMEM((NZ, ROWS, 4 * ROWS), F32),
            pltpu.VMEM((ROWS, PROJ), F32),
            pltpu.VMEM((ROWS, 1), F32),
            pltpu.VMEM((ROWS, 1), jnp.int32),
            pltpu.VMEM((ROWS, 128), F32),
            pltpu.VMEM((ROWS, 128), F32),
            pltpu.VMEM((32, 1, ROWS), F32),
            pltpu.VMEM((ROWS, PROJ), F32),
            pltpu.VMEM((ROWS, HID // 2), BF16),
            pltpu.VMEM((HID // 2, 2 * ROWS), BF16),
            pltpu.VMEM((2, ROWS, PROJ), BF16),
            pltpu.VMEM((4, 4, 64, PROJ), F32),
            pltpu.VMEM((4, 4, 64, PROJ), BF16),
            pltpu.VMEM((4, 3, 64, PROJ), BF16),
            pltpu.VMEM((4, 4, 16, PROJ), F32),
            pltpu.VMEM((4, 3, 16, PROJ), F32),
            pltpu.VMEM((4, 16, PROJ), F32),
            pltpu.VMEM((7, 16, 256), F32),
            pltpu.SemaphoreType.REGULAR,
            dma((2, 4, 3)), dma((2, 4, 3)),
            dma((2, 4)), dma((2, 4)),
            dma((2, 5, 2)), dma((2, 5, 2)),
            dma((32,)), dma((32,)),
            dma((2,)), dma((2,)),
            dma((4, 3)), dma((4, 3)),
            dma((4, 3)), dma((4, 3)),
            dma((7,)), dma((7,)),
            dma((7,)), dma((7,)),
            dma((4, 3)), dma((4, 3)),
            dma((4, 3)), dma((4, 3)),
            dma((4, 4)), dma((4, 4)),
        ],
        compiler_params=pltpu.CompilerParams(
            collective_id=0, has_side_effects=True, vmem_limit_bytes=44 << 20
        ),
        name="ntxent",
    )(features[0], head_weight, pairs)
    inputs = [pltpu.with_memory_space_constraint(a, pltpu.VMEM) for a in (pos, lse, dz, head)]
    pos, lse, dz, head = pl.pallas_call(
        finish,
        out_shape=(
            jax.ShapeDtypeStruct((1, ROWS), F32),
            jax.ShapeDtypeStruct((1, ROWS), F32),
            jax.ShapeDtypeStruct((ROWS, PROJ), F32),
            jax.ShapeDtypeStruct((HID, PROJ), F32),
        ),
        in_specs=[vmem] * 4,
        out_specs=(pl.BlockSpec(memory_space=pl.ANY),) * 4,
        scratch_shapes=[pltpu.VMEM((HID, PROJ), F32), dma((11,))],
        compiler_params=pltpu.CompilerParams(vmem_limit_bytes=16 << 20),
        name="finish",
    )(*inputs)
    return pos, lse, dz[None], head


def solution(mesh):
    in_specs = (P("group", "blk", None), P(), P("group", "blk"))
    out_specs = (P("group", "blk"), P("group", "blk"), P("group", "blk", None), P())
    return jax.shard_map(
        on_device, mesh=mesh, in_specs=in_specs, out_specs=out_specs, check_vma=False
    )
```

```python
import functools

import jax
import jax.numpy as jnp
from jax import lax
from jax.experimental import pallas as pl
from jax.experimental.pallas import tpu as pltpu
from jax.sharding import PartitionSpec as P

MESH = pl.DeviceIdType.MESH
F32 = jnp.float32
BF16 = jnp.bfloat16

HID = 2048
PROJ = 512
ROWS = 256
NZ = 8
NA = (176, 160)
KCUTS = 4
INV_TEMP = 10.0
LOG2E = 1.4426950408889634

LAST = (
    (1, 0, 0, 64),
    (0, 0, 64, 112),
    (0, 0, 176, 80),
    (1, 1, 0, 96),
    (0, 1, 176, 80),
    (1, 1, 96, 80),
)
LATE_Y = ((1, 0, 96), (1, 96, 64), (0, 0, 176))


def kernel(
    feat_hbm, w_hbm, pairs_hbm,
    pos_ref, lse_ref, dz_ref, head_ref,
    feat_ref, w_ref, pairs_ref, load_sem,
    ub_all, e_all, u_s, inv_s, pcol_s, den_s, pos_s, rden_all, acc_s,
    f_sib, f_t, dzb, pf, sb1, r1, qf, r2, zb, r3, in_sem,
    z_send, z_recv, l_send, l_recv, lc_send, lc_recv, ly_send, ly_recv, y_send, y_recv, c_send, c_recv, d_send, d_recv,
    x_send, x_recv, s1_send, s1_recv, s2_send, s2_recv, s3_send, s3_recv,
    g3_send, g3_recv, g2_send, g2_recv, g1_send, g1_recv, gc_send, gc_recv,
):
    blk = lax.axis_index("blk")
    grp = lax.axis_index("group")
    z, yl, c = blk // 4, lax.rem(blk // 2, 2), lax.rem(blk, 2)
    yh, x = grp // 4, lax.rem(grp, 4)
    y = yh * 2 + yl

    def dev(z_, y_, c_, x_):
        return ((z_ * 2 + lax.rem(y_, 2)) * 2 + c_, (y_ // 2) * 4 + x_)

    def copy(src, dst, ssem, rsem, to):
        return pltpu.make_async_remote_copy(
            src_ref=src, dst_ref=dst, send_sem=ssem, recv_sem=rsem,
            device_id=to, device_id_type=MESH,
        )

    sib = dev(z, y, 1 - c, x)
    ynb = (blk + 2 - 4 * yl, grp)

    barrier = pltpu.get_barrier_semaphore()
    ring = (
        dev(z, y, c, lax.rem(x + 1, 4)),
        dev(z, y, c, lax.rem(x + 3, 4)),
        dev(z, lax.rem(y + 1, 4), c, x),
        dev(z, lax.rem(y + 3, 4), c, x),
    )
    znext = (dev(lax.rem(z + 1, NZ), y, c, x), dev(lax.rem(z + NZ - 1, NZ), y, c, x))
    for to in znext + (sib,) + ring:
        pl.semaphore_signal(barrier, inc=1, device_id=to, device_id_type=MESH)

    def kcut(k):
        return slice(k * (HID // KCUTS), (k + 1) * (HID // KCUTS))

    loads = []
    for k in range(KCUTS):
        loads.append(pltpu.make_async_copy(feat_hbm.at[:, kcut(k)], feat_ref.at[:, kcut(k)], load_sem.at[2 * k]))
        loads.append(pltpu.make_async_copy(w_hbm.at[kcut(k), :], w_ref.at[kcut(k), :], load_sem.at[2 * k + 1]))
    loads.append(pltpu.make_async_copy(pairs_hbm, pairs_ref, load_sem.at[2 * KCUTS]))
    for cp in loads:
        cp.start()

    zz = jnp.zeros((ROWS, PROJ), F32)
    for k in range(KCUTS):
        for cp in loads[2 * k : 2 * k + 2]:
            cp.wait()
        zz += jnp.dot(feat_ref[:, kcut(k)], w_ref[kcut(k), :], preferred_element_type=F32)
    loads[-1].wait()
    inv = lax.rsqrt(jnp.sum(zz * zz, axis=1, keepdims=True) + 1e-06)
    u = zz * inv
    inv_s[...] = inv
    u_s[...] = u
    row0 = pl.multiple_of((yl * 2 + c) * ROWS, ROWS)
    ub_all[z, pl.ds(row0, ROWS), :] = u.astype(BF16)
    pl.semaphore_wait(barrier, 7)

    def origin(dr, s):
        return lax.rem(z + NZ + (-s if dr == 0 else s), NZ)

    def rows_of(yl_, c_, off, n):
        return pl.ds(pl.multiple_of((yl_ * 2 + c_) * ROWS + off, 16), n)

    def piece(zo, yl_, c_, off, n):
        return ub_all.at[zo, rows_of(yl_, c_, off, n), :]

    def z_ref(dr, kind, zo):
        na = NA[dr]
        return piece(zo, 1 - yl if kind == 2 else yl, c, *((na, ROWS - na) if kind else (0, na)))

    def z_copy(dr, s, kind):
        ref = z_ref(dr, kind, origin(dr, s))
        return copy(ref, ref, z_send.at[dr, s, kind], z_recv.at[dr, s, kind], znext[dr])

    def z_arrived(dr, s, kind):
        ref = z_ref(dr, kind, origin(dr, s + 1))
        return copy(ref, ref, z_send.at[dr, s, kind], z_recv.at[dr, s, kind], znext[dr])

    def last_ref(i, hops, c_):
        dr, other, off, n = LAST[i]
        return piece(origin(dr, hops), 1 - yl if other else yl, c_, off, n)

    def last_copy(i):
        ref = last_ref(i, 3, c)
        return copy(ref, ref, l_send.at[i], l_recv.at[i], znext[LAST[i][0]])

    def last_arrived(i):
        ref = last_ref(i, 4, c)
        return copy(ref, ref, l_send.at[i], l_recv.at[i], znext[LAST[i][0]])

    def last_chip_copy(i):
        ref = last_ref(i, 4, c)
        return copy(ref, ref, lc_send.at[i], lc_recv.at[i], sib)

    def last_chip_arrived(i):
        ref = last_ref(i, 4, 1 - c)
        return copy(ref, ref, lc_send.at[i], lc_recv.at[i], sib)

    def late_y(i, mine_):
        dr, off, n = LATE_Y[i]
        ref = piece(origin(dr, 3), yl if mine_ else 1 - yl, c, off, n)
        return copy(ref, ref, ly_send.at[i], ly_recv.at[i], ynb)

    def y_ref(dr, s, yl_):
        if s == 0:
            return piece(z, yl_, c, *((NA[1], ROWS - NA[1]) if dr == 0 else (0, NA[1])))
        return piece(origin(dr, s), yl_, c, 0, NA[dr])

    def y_copy(dr, s):
        ref = y_ref(dr, s, yl)
        return copy(ref, ref, y_send.at[dr, s], y_recv.at[dr, s], ynb)

    def y_arrived(dr, s):
        ref = y_ref(dr, s, 1 - yl)
        return copy(ref, ref, y_send.at[dr, s], y_recv.at[dr, s], ynb)

    def c_ref(dr, s, other, c_):
        return piece(origin(dr, s), 1 - yl if other else yl, c_, 0, ROWS)

    def c_copy(dr, s, other):
        ref = c_ref(dr, s, other, c)
        return copy(ref, ref, c_send.at[dr, s, other], c_recv.at[dr, s, other], sib)

    def c_arrived(dr, s, other):
        ref = c_ref(dr, s, other, 1 - c)
        return copy(ref, ref, c_send.at[dr, s, other], c_recv.at[dr, s, other], sib)

    sent = []

    def go(cp):
        cp.start()
        sent.append(cp)

    def flush():
        for cp in sent:
            cp.wait_send()
        sent.clear()

    go(y_copy(0, 0))
    for kind in (0, 1):
        for dr in (0, 1):
            go(z_copy(dr, 0, kind))
    go(y_copy(1, 0))
    go(c_copy(0, 0, 0))
    for to in ring:
        pl.semaphore_signal(in_sem, inc=1, device_id=to, device_id_type=MESH)
    mine = pl.multiple_of(c * (HID // 2), HID // 2)
    theirs = pl.multiple_of((1 - c) * (HID // 2), HID // 2)
    xcp = copy(feat_ref.at[:, pl.ds(theirs, HID // 2)], f_sib, x_send.at[0], x_recv.at[0], sib)
    go(xcp)

    pcol_s[...] = jnp.broadcast_to(pairs_ref[...], (128, ROWS)).T[:, :1]
    den_s[...] = jnp.zeros_like(den_s)
    pos_s[...] = jnp.zeros_like(pos_s)
    own_row = blk * ROWS + lax.broadcasted_iota(jnp.int32, (ROWS, 1), 0)

    def scores(zo, j):
        block = ub_all[zo, pl.ds(pl.multiple_of(j * ROWS, ROWS), ROWS), :]
        mine_ub = ub_all[z, pl.ds(row0, ROWS), :]
        s = lax.dot_general(
            mine_ub, block, (((1,), (1,)), ((), ())), preferred_element_type=F32
        )
        cols = (zo * 4 + j) * ROWS + lax.broadcasted_iota(jnp.int32, (ROWS, ROWS), 1)
        e = jnp.where(cols == own_row, 0.0, jnp.exp2(s * (INV_TEMP * LOG2E)))
        e_all[zo, :, pl.ds(pl.multiple_of(j * ROWS, ROWS), ROWS)] = e
        p = jnp.where(cols == pcol_s[...], s, 0.0)
        den_s[...] += e[:, :128] + e[:, 128:]
        pos_s[...] += p[:, :128] + p[:, 128:]

    def scores_of(zo):
        def body(j, carry):
            scores(zo, j)
            return carry

        lax.fori_loop(0, 4, body, 0)

    y_arrived(0, 0).wait_recv()
    for dr in (0, 1):
        go(z_copy(dr, 0, 2))
    f_t[:, :ROWS] = feat_ref[:, pl.ds(mine, HID // 2)].T
    y_arrived(1, 0).wait_recv()
    go(c_copy(0, 0, 1))
    xcp.wait_recv()
    f_t[:, ROWS:] = f_sib[...].T

    def scores_pair(dr, s, other):
        c_arrived(dr, s, other).wait_recv()

        def body(k, carry):
            scores(origin(dr, s), (1 - yl if other else yl) * 2 + k)
            return carry

        lax.fori_loop(0, 2, body, 0)

    for s in (1, 2, 3):
        last = s == 3
        drs = (0,) if s == 1 else (0, 1)
        for dr in (0, 1):
            z_arrived(dr, s - 1, 0).wait_recv()
            if last:
                go(last_copy(1 - dr))
            else:
                go(z_copy(dr, s, 0))
                go(y_copy(dr, s))
        if last:
            for i in range(3):
                go(late_y(i, True))
        for dr in drs:
            scores_pair(dr, s - 1, 0)
        for dr in (0, 1):
            z_arrived(dr, s - 1, 1).wait_recv()
            if not last:
                go(z_copy(dr, s, 1))
            elif dr == 0:
                go(last_copy(2))
            go(c_copy(dr, s, 0))
        if s > 1:
            for dr in (0, 1):
                y_arrived(dr, s - 1).wait_recv()
                go(c_copy(dr, s - 1, 1))
        for dr in (0, 1):
            z_arrived(dr, s - 1, 2).wait_recv()
            if not last:
                go(z_copy(dr, s, 2))
            elif dr == 0:
                go(last_copy(4))
        if last:
            late_y(0, False).wait_recv()
            go(last_copy(3))
            scores_pair(0, 2, 1)
            late_y(1, False).wait_recv()
            go(last_copy(5))
            go(c_copy(1, 3, 1))
            scores_pair(1, 2, 1)
        else:
            for dr in drs:
                scores_pair(dr, s - 1, 1)
    for dr in (0, 1):
        scores_pair(dr, 3, 0)
    for i in (0, 1, 2):
        last_arrived(i).wait_recv()
        go(last_chip_copy(i))
    scores_pair(1, 3, 1)
    late_y(2, False).wait_recv()
    go(c_copy(0, 3, 1))
    far = origin(0, 4)
    scores(far, yl * 2 + c)
    for i in (3, 4):
        last_arrived(i).wait_recv()
        go(last_chip_copy(i))
    scores_pair(0, 3, 1)
    last_arrived(5).wait_recv()
    go(last_chip_copy(5))
    scores(far, (1 - yl) * 2 + c)
    for i in (0, 1, 2):
        last_chip_arrived(i).wait_recv()
    scores(far, yl * 2 + 1 - c)
    for i in (3, 4, 5):
        last_chip_arrived(i).wait_recv()
    scores(far, (1 - yl) * 2 + 1 - c)

    den = jnp.sum(den_s[...], axis=1, keepdims=True)
    r_own = 1.0 / den
    rden_all[blk] = jnp.broadcast_to(r_own, (ROWS, 128)).T[:1, :]

    def d_copy(dz_, k):
        to_blk = lax.rem(z + dz_, NZ) * 4 + lax.rem(yl + k // 2, 2) * 2 + lax.rem(c + k % 2, 2)
        i = dz_ * 4 + k
        return copy(
            rden_all.at[blk], rden_all.at[blk], d_send.at[i], d_recv.at[i], (to_blk, grp)
        )

    def d_arrived(dz_, k):
        i = dz_ * 4 + k
        from_blk = (
            lax.rem(z + NZ - dz_, NZ) * 4
            + lax.rem(yl + k // 2, 2) * 2
            + lax.rem(c + k % 2, 2)
        )
        ref = rden_all.at[from_blk]
        return copy(ref, ref, d_send.at[i], d_recv.at[i], (blk, grp))

    for dz_ in (4, 3, 5, 2, 6, 1, 7, 0):
        for k in range(4):
            if dz_ or k:
                go(d_copy(dz_, k))

    pl.semaphore_wait(in_sem, 4)
    lse_ref[...] = jnp.broadcast_to(jnp.log(den), (ROWS, 128)).T[:1, :]
    pos = jnp.sum(pos_s[...], axis=1, keepdims=True) * INV_TEMP
    pos_ref[...] = jnp.broadcast_to(pos, (ROWS, 128)).T[:1, :]

    for n, dz_ in enumerate((0, 1, 7, 2, 6, 3, 5, 4)):
        for k in range(4):
            if dz_ or k:
                d_arrived(dz_, k).wait_recv()
        zo = lax.rem(z + NZ - dz_, NZ)
        parts = []
        for j in range(4):
            cols = (zo * 4 + j) * ROWS + lax.broadcasted_iota(jnp.int32, (ROWS, ROWS), 1)
            e = e_all[zo, :, j * ROWS : (j + 1) * ROWS]
            h = e * (r_own + rden_all[zo * 4 + j]) - jnp.where(cols == pcol_s[...], 2.0, 0.0)
            parts.append(h.astype(BF16))
        g = jnp.dot(
            jnp.concatenate(parts, axis=1), ub_all[zo], preferred_element_type=F32
        )
        if n == 0:
            acc_s[...] = g
        else:
            acc_s[...] += g

    slope = acc_s[...] * INV_TEMP
    u = u_s[...]
    dz = inv_s[...] * (slope - u * jnp.sum(u * slope, axis=1, keepdims=True))
    dz_ref[...] = dz
    dzb[0] = dz.astype(BF16)
    xcp = copy(dzb.at[0], dzb.at[1], x_send.at[1], x_recv.at[1], sib)
    go(xcp)
    xcp.wait_recv()

    def along(t, first, d):
        if (t % 2 == 0) == first:
            return dev(z, y, c, lax.rem(x + d, 4))
        return dev(z, lax.rem(y + d, 4), c, x)

    def place(t, first):
        return x if (t % 2 == 0) == first else y

    def s1_copy(t, d):
        j = lax.rem(place(t, True) + d, 4)
        return copy(sb1.at[t, j], r1.at[t, d - 1], s1_send.at[t, d - 1], s1_recv.at[t, d - 1], along(t, True, d))

    def s2_copy(t, d):
        j = lax.rem(place(t, False) + d, 4)
        return copy(qf.at[t, j], r2.at[t, d - 1], s2_send.at[t, d - 1], s2_recv.at[t, d - 1], along(t, False, d))

    def out_rows(t, a, b, n):
        start = c * (HID // 2) + t * 256 + a * 64 + b * 16
        return pl.ds(pl.multiple_of(start, 16), n)

    def zcols(j):
        return pl.ds(pl.multiple_of(lax.rem(j, 2) * 256, 256), 256)

    def zpeer(d):
        return dev(lax.rem(z + d, NZ), y, c, x)

    def s3_copy(d):
        j = lax.rem(z + d, NZ)
        return copy(zb.at[j // 2, :, zcols(j)], r3.at[d - 1], s3_send.at[d - 1], s3_recv.at[d - 1], zpeer(d))

    def zrows(j):
        t = j // 2
        odd = lax.rem(t, 2)
        return out_rows(t, x + odd * (y - x), y + odd * (x - y), 16)

    def g3_copy(d, mine_=True):
        j = z if mine_ else lax.rem(z + NZ - d, NZ)
        ref = head_ref.at[zrows(j), zcols(j)]
        return copy(ref, ref, g3_send.at[d - 1], g3_recv.at[d - 1], zpeer(d))

    def g2_copy(t, d, mine_=True):
        b = place(t, False)
        ref = head_ref.at[out_rows(t, place(t, True), b if mine_ else lax.rem(b + 4 - d, 4), 16), :]
        return copy(ref, ref, g2_send.at[t, d - 1], g2_recv.at[t, d - 1], along(t, False, d))

    def g1_copy(t, d, mine_=True):
        a = place(t, True)
        ref = head_ref.at[out_rows(t, a if mine_ else lax.rem(a + 4 - d, 4), 0, 64), :]
        return copy(ref, ref, g1_send.at[t, d - 1], g1_recv.at[t, d - 1], along(t, True, d))

    def gc_copy(t, d):
        a = place(t, True)
        ref = head_ref.at[out_rows(t, lax.rem(a + 4 - d, 4), 0, 64), :]
        return copy(ref, ref, gc_send.at[t, d], gc_recv.at[t, d], sib)

    def gc_arrived(t, d):
        start = (1 - c) * (HID // 2) + t * 256 + lax.rem(place(t, True) + 4 - d, 4) * 64
        ref = head_ref.at[pl.ds(pl.multiple_of(start, 64), 64), :]
        return copy(ref, ref, gc_send.at[t, d], gc_recv.at[t, d], sib)

    D3, D7 = (2, 1, 3), (4, 3, 5, 2, 6, 1, 7)

    def stage1(t):
        dzs = jnp.concatenate([dzb[0], dzb[1]], axis=0)
        part = jnp.dot(f_t[t * 256 : (t + 1) * 256, :], dzs, preferred_element_type=F32)
        pf[t] = part.reshape(4, 64, PROJ)
        sb1[t] = part.astype(BF16).reshape(4, 64, PROJ)
        for d in D3:
            go(s1_copy(t, d))

    def stage2(t):
        for d in D3:
            s1_copy(t, d).wait_recv()
        total = pf[t, place(t, True)]
        for d in range(3):
            total = total + r1[t, d].astype(F32)
        qf[t] = total.reshape(4, 16, PROJ)
        for d in D3:
            go(s2_copy(t, d))

    def stage3():
        for t in range(4):
            for d in D3:
                s2_copy(t, d).wait_recv()
            zb[t] = qf[t, place(t, False)] + r2[t, 0] + r2[t, 1] + r2[t, 2]
        for d in D7:
            go(s3_copy(d))

    def stage4():
        total = zb[z // 2, :, zcols(z)]
        for d in D7:
            s3_copy(d).wait_recv()
        for d in range(7):
            total = total + r3[d]
        head_ref[zrows(z), zcols(z)] = total.astype(BF16)
        for d in D7:
            go(g3_copy(d))

    def stage5():
        for d in D7:
            g3_copy(d, False).wait_recv()
        for t in range(4):
            for d in D3:
                go(g2_copy(t, d))

    def stage6(t):
        for d in D3:
            g2_copy(t, d, False).wait_recv()
        for d in D3:
            go(g1_copy(t, d))
        go(gc_copy(t, 0))

    def stage7(t):
        for d in D3:
            g1_copy(t, d, False).wait_recv()
            go(gc_copy(t, d))

    for t in range(4):
        stage1(t)
    for t in range(4):
        stage2(t)
    stage3()
    flush()
    stage4()
    stage5()
    flush()
    for t in range(4):
        stage6(t)
    for t in range(4):
        stage7(t)
    for t in range(4):
        for d in range(4):
            gc_arrived(t, d).wait_recv()
    flush()


def finish(pos_in, lse_in, dz_in, head_in, pos_ref, lse_ref, dz_ref, head_ref, buf, sem):
    copies = [
        pltpu.make_async_copy(dz_in, dz_ref, sem.at[0]),
        pltpu.make_async_copy(pos_in, pos_ref, sem.at[1]),
        pltpu.make_async_copy(lse_in, lse_ref, sem.at[2]),
    ]
    for cp in copies:
        cp.start()
    for i in range(8):
        rows = slice(i * 256, (i + 1) * 256)
        buf[rows, :] = head_in[rows, :].astype(F32)
        cp = pltpu.make_async_copy(buf.at[rows, :], head_ref.at[rows, :], sem.at[3 + i])
        cp.start()
        copies.append(cp)
    for cp in copies:
        cp.wait()


def on_device(features, head_weight, pairs):
    vmem = pl.BlockSpec(memory_space=pltpu.VMEM)
    dma = pltpu.SemaphoreType.DMA
    pos, lse, dz, head = pl.pallas_call(
        kernel,
        out_shape=(
            pltpu.VMEM((1, ROWS), F32),
            pltpu.VMEM((1, ROWS), F32),
            pltpu.VMEM((ROWS, PROJ), F32),
            pltpu.VMEM((HID, PROJ), BF16),
        ),
        in_specs=[pl.BlockSpec(memory_space=pltpu.HBM)] * 3,
        out_specs=(vmem,) * 4,
        scratch_shapes=[
            pltpu.VMEM((ROWS, HID), BF16),
            pltpu.VMEM((HID, PROJ), BF16),
            pltpu.VMEM((1, ROWS), jnp.int32),
            dma((2 * KCUTS + 1,)),
            pltpu.VMEM((NZ, 4 * ROWS, PROJ), BF16),
            pltpu.VMEM((NZ, ROWS, 4 * ROWS), F32),
            pltpu.VMEM((ROWS, PROJ), F32),
            pltpu.VMEM((ROWS, 1), F32),
            pltpu.VMEM((ROWS, 1), jnp.int32),
            pltpu.VMEM((ROWS, 128), F32),
            pltpu.VMEM((ROWS, 128), F32),
            pltpu.VMEM((32, 1, ROWS), F32),
            pltpu.VMEM((ROWS, PROJ), F32),
            pltpu.VMEM((ROWS, HID // 2), BF16),
            pltpu.VMEM((HID // 2, 2 * ROWS), BF16),
            pltpu.VMEM((2, ROWS, PROJ), BF16),
            pltpu.VMEM((4, 4, 64, PROJ), F32),
            pltpu.VMEM((4, 4, 64, PROJ), BF16),
            pltpu.VMEM((4, 3, 64, PROJ), BF16),
            pltpu.VMEM((4, 4, 16, PROJ), F32),
            pltpu.VMEM((4, 3, 16, PROJ), F32),
            pltpu.VMEM((4, 16, PROJ), F32),
            pltpu.VMEM((7, 16, 256), F32),
            pltpu.SemaphoreType.REGULAR,
            dma((2, 3, 3)), dma((2, 3, 3)),
            dma((6,)), dma((6,)),
            dma((6,)), dma((6,)),
            dma((3,)), dma((3,)),
            dma((2, 3)), dma((2, 3)),
            dma((2, 4, 2)), dma((2, 4, 2)),
            dma((32,)), dma((32,)),
            dma((2,)), dma((2,)),
            dma((4, 3)), dma((4, 3)),
            dma((4, 3)), dma((4, 3)),
            dma((7,)), dma((7,)),
            dma((7,)), dma((7,)),
            dma((4, 3)), dma((4, 3)),
            dma((4, 3)), dma((4, 3)),
            dma((4, 4)), dma((4, 4)),
        ],
        compiler_params=pltpu.CompilerParams(
            collective_id=0, has_side_effects=True, vmem_limit_bytes=44 << 20
        ),
        name="ntxent",
    )(*[pltpu.with_memory_space_constraint(a, pltpu.HBM) for a in (features[0], head_weight, pairs)])
    inputs = [pltpu.with_memory_space_constraint(a, pltpu.VMEM) for a in (pos, lse, dz, head)]
    pos, lse, dz, head = pl.pallas_call(
        finish,
        out_shape=(
            jax.ShapeDtypeStruct((1, ROWS), F32),
            jax.ShapeDtypeStruct((1, ROWS), F32),
            jax.ShapeDtypeStruct((ROWS, PROJ), F32),
            jax.ShapeDtypeStruct((HID, PROJ), F32),
        ),
        in_specs=[vmem] * 4,
        out_specs=(pl.BlockSpec(memory_space=pl.ANY),) * 4,
        scratch_shapes=[pltpu.VMEM((HID, PROJ), F32), dma((11,))],
        compiler_params=pltpu.CompilerParams(vmem_limit_bytes=16 << 20),
        name="finish",
    )(*inputs)
    return pos, lse, dz[None], head


def solution(mesh):
    in_specs = (P("group", "blk", None), P(), P("group", "blk"))
    out_specs = (P("group", "blk"), P("group", "blk"), P("group", "blk", None), P())
    return jax.shard_map(
        on_device, mesh=mesh, in_specs=in_specs, out_specs=out_specs, check_vma=False
    )
```

```python
import functools

import jax
import jax.numpy as jnp
from jax import lax
from jax.experimental import pallas as pl
from jax.experimental.pallas import tpu as pltpu
from jax.sharding import PartitionSpec as P

MESH = pl.DeviceIdType.MESH
F32 = jnp.float32
BF16 = jnp.bfloat16

HID = 2048
PROJ = 512
ROWS = 256
NZ = 8
LOW = True
CUT = 64
KCUTS = 4
INV_TEMP = 10.0
LOG2E = 1.4426950408889634


def kernel(
    feat_hbm, w_hbm, pairs_hbm,
    pos_ref, lse_ref, dz_ref, head_ref,
    feat_ref, w_ref, pairs_ref, load_sem,
    ub_all, ub_r, e_all, u_s, inv_s, pcol_s, den_s, pos_s, den_mine, den_all, den_o, pos_x, pos_y,
    acc_s, feat_o, pairs_o, f_sib, f_t, dzh, dzl, dzx, pf, sb1, r1, qf, r2, zb, r3, in_sem,
    z_send, z_recv, y_send, y_recv, fy_send, fy_recv, c_send, c_recv, fc_send, fc_recv,
    d_send, d_recv, x_send, x_recv, s1_send, s1_recv, s2_send, s2_recv, s3_send, s3_recv,
    g3_send, g3_recv, g2_send, g2_recv, g1_send, g1_recv, gc_send, gc_recv,
):
    blk = lax.axis_index("blk")
    grp = lax.axis_index("group")
    z, yl, c = blk // 4, lax.rem(blk // 2, 2), lax.rem(blk, 2)
    yh, x = grp // 4, lax.rem(grp, 4)
    y = yh * 2 + yl

    def dev(z_, y_, c_, x_):
        return ((z_ * 2 + lax.rem(y_, 2)) * 2 + c_, (y_ // 2) * 4 + x_)

    def copy(src, dst, ssem, rsem, to):
        return pltpu.make_async_remote_copy(
            src_ref=src, dst_ref=dst, send_sem=ssem, recv_sem=rsem,
            device_id=to, device_id_type=MESH,
        )

    sib = dev(z, y, 1 - c, x)
    ynb = (blk + 2 - 4 * yl, grp)

    barrier = pltpu.get_barrier_semaphore()
    ring = (
        dev(z, y, c, lax.rem(x + 1, 4)),
        dev(z, y, c, lax.rem(x + 3, 4)),
        dev(z, lax.rem(y + 1, 4), c, x),
        dev(z, lax.rem(y + 3, 4), c, x),
    )
    znext = (dev(lax.rem(z + 1, NZ), y, c, x), dev(lax.rem(z + NZ - 1, NZ), y, c, x))
    for to in znext + (sib,) + ring:
        pl.semaphore_signal(barrier, inc=1, device_id=to, device_id_type=MESH)

    def kcut(k):
        return slice(k * (HID // KCUTS), (k + 1) * (HID // KCUTS))

    loads = []
    for k in range(KCUTS):
        loads.append(pltpu.make_async_copy(feat_hbm.at[:, kcut(k)], feat_ref.at[:, kcut(k)], load_sem.at[2 * k]))
        loads.append(pltpu.make_async_copy(w_hbm.at[kcut(k), :], w_ref.at[kcut(k), :], load_sem.at[2 * k + 1]))
    loads.append(pltpu.make_async_copy(pairs_hbm, pairs_ref, load_sem.at[2 * KCUTS]))
    for cp in loads:
        cp.start()

    zz = jnp.zeros((ROWS, PROJ), F32)
    for k in range(KCUTS):
        for cp in loads[2 * k : 2 * k + 2]:
            cp.wait()
        zz += jnp.dot(feat_ref[:, kcut(k)], w_ref[kcut(k), :], preferred_element_type=F32)
    loads[-1].wait()
    inv = lax.rsqrt(jnp.sum(zz * zz, axis=1, keepdims=True) + 1e-06)
    u = zz * inv
    inv_s[:ROWS] = inv
    u_s[:ROWS] = u
    ub = u.astype(BF16)
    ub_r[0] = ub
    ub_all[z, pl.ds(pl.multiple_of(c * ROWS, ROWS), ROWS), :] = ub
    pl.semaphore_wait(barrier, 7)

    def origin(dr, s):
        return lax.rem(z + NZ + (-s if dr == 0 else s), NZ)

    def piece(zo, c_, off, n):
        return ub_all.at[zo, pl.ds(pl.multiple_of(c_ * ROWS + off, 16), n), :]

    def z_copy(dr, s, p):
        ref = piece(origin(dr, s), c, p * CUT, CUT)
        return copy(ref, ref, z_send.at[dr, s, p], z_recv.at[dr, s, p], znext[dr])

    def z_arrived(dr, s, p):
        ref = piece(origin(dr, s + 1), c, p * CUT, CUT)
        return copy(ref, ref, z_send.at[dr, s, p], z_recv.at[dr, s, p], znext[dr])

    def c_ref(dr, s, c_):
        return piece(origin(dr, s), c_, *((dr * 128, 128) if s == 4 else (0, ROWS)))

    def c_copy(dr, s):
        ref = c_ref(dr, s, c)
        return copy(ref, ref, c_send.at[dr, s], c_recv.at[dr, s], sib)

    def c_arrived(dr, s):
        ref = c_ref(dr, s, 1 - c)
        return copy(ref, ref, c_send.at[dr, s], c_recv.at[dr, s], sib)

    sent = []

    def go(cp):
        cp.start()
        sent.append(cp)

    def flush():
        for cp in sent:
            cp.wait_send()
        sent.clear()

    yub = copy(ub_r.at[0], ub_r.at[1], y_send.at[0], y_recv.at[0], ynb)
    ypairs = copy(pairs_ref, pairs_o, y_send.at[1], y_recv.at[1], ynb)
    go(yub)
    go(ypairs)
    for p in range(4):
        for dr in (0, 1):
            go(z_copy(dr, 0, p))
    go(c_copy(0, 0))

    def fy_copy(k):
        return copy(feat_ref.at[:, kcut(k)], feat_o.at[:, kcut(k)], fy_send.at[k], fy_recv.at[k], ynb)

    for k in range(KCUTS):
        go(fy_copy(k))
    for to in ring:
        pl.semaphore_signal(in_sem, inc=1, device_id=to, device_id_type=MESH)

    half = HID // 2
    cut = HID // KCUTS
    mine = pl.multiple_of(c * half, half)
    theirs = pl.multiple_of((1 - c) * half, half)
    xcp = copy(feat_ref.at[:, pl.ds(theirs, half)], f_sib.at[0], x_send.at[0], x_recv.at[0], sib)
    go(xcp)

    def fc_copy(q):
        cols = pl.ds(pl.multiple_of((1 - c) * half + q * cut, cut), cut)
        dst = f_sib.at[1, :, q * cut : (q + 1) * cut]
        return copy(feat_o.at[:, cols], dst, fc_send.at[q], fc_recv.at[q], sib)

    den_s[...] = jnp.zeros_like(den_s)
    pos_s[...] = jnp.zeros_like(pos_s)
    sub = lax.broadcasted_iota(jnp.int32, (2 * ROWS, 1), 0)
    other_blk = blk + 2 - 4 * yl
    own_row = jnp.where(sub < ROWS, blk * ROWS, other_blk * ROWS - ROWS) + sub

    def column(row):
        return jnp.broadcast_to(row, (128, ROWS)).T[:, :1]

    def cols_of(zo, k):
        first = (zo * 4 + yl * 2 + k) * ROWS
        return first + lax.broadcasted_iota(jnp.int32, (2 * ROWS, ROWS), 1)

    def scores(zo, k):
        lanes = pl.ds(pl.multiple_of(k * ROWS, ROWS), ROWS)
        s = lax.dot_general(
            ub_r[...].reshape(2 * ROWS, PROJ), ub_all[zo, lanes, :],
            (((1,), (1,)), ((), ())), preferred_element_type=F32,
        )
        cols = cols_of(zo, k)
        e = jnp.where(cols == own_row, 0.0, jnp.exp2(s * (INV_TEMP * LOG2E)))
        e_all[zo, :, lanes] = e
        p = jnp.where(cols == pcol_s[...], s, 0.0)
        den_s[...] += e[:, :128] + e[:, 128:]
        pos_s[...] += p[:, :128] + p[:, 128:]

    def other_z(k):
        fy_copy(k).wait_recv()
        part = jnp.dot(feat_o[:, kcut(k)], w_ref[kcut(k), :], preferred_element_type=F32)
        if k == 0:
            u_s[ROWS:] = part
        else:
            u_s[ROWS:] += part

    for s in (1, 2, 3):
        for p in range(4):
            for dr in (0, 1):
                z_arrived(dr, s - 1, p).wait_recv()
                if s < 3 or p // 2 == dr:
                    go(z_copy(dr, s, p))
                if p == 3:
                    go(c_copy(dr, s))
            if s == 1:
                if p == 1:
                    f_t[:, :ROWS] = feat_ref[:, pl.ds(mine, half)].T
                if p == 2:
                    xcp.wait_recv()
                    f_t[:, 2 * ROWS : 3 * ROWS] = f_sib[0].T
                if p == 3:
                    yub.wait_recv()
                    ypairs.wait_recv()
                    pcol_s[:ROWS] = column(pairs_ref[...])
                    pcol_s[ROWS:] = column(pairs_o[...])
                    scores(z, c)
                    c_arrived(0, 0).wait_recv()
                    scores(z, 1 - c)
            else:
                dr = p % 2
                if p >= 2:
                    c_arrived(dr, s - 1).wait_recv()
                scores(origin(dr, s - 1), c if p < 2 else 1 - c)
    for dr in (0, 1):
        scores(origin(dr, 3), c)
    other_z(0)
    for dr in (0, 1):
        c_arrived(dr, 3).wait_recv()
        scores(origin(dr, 3), 1 - c)
    far = origin(0, 4)
    for dr in (0, 1):
        for p in (2 * dr, 2 * dr + 1):
            z_arrived(dr, 3, p).wait_recv()
        go(c_copy(dr, 4))
    scores(far, c)
    for dr in (0, 1):
        c_arrived(dr, 4).wait_recv()
    scores(far, 1 - c)

    sums = jnp.broadcast_to(jnp.sum(den_s[...], axis=1, keepdims=True), (2 * ROWS, 128)).T
    den_mine[0] = sums[:1, :ROWS]
    den_mine[1] = sums[:1, ROWS:]
    den_all[0, z * 2 + c] = sums[:1, :ROWS]

    def d_copy(dz_, dy, dc):
        to_blk = lax.rem(z + dz_, NZ) * 4 + lax.rem(yl + dy, 2) * 2 + lax.rem(c + dc, 2)
        i = dz_ * 4 + dy * 2 + dc
        return copy(
            den_mine.at[dy], den_all.at[dy, z * 2 + c], d_send.at[i], d_recv.at[i], (to_blk, grp)
        )

    def d_arrived(dz_, dy, dc):
        i = dz_ * 4 + dy * 2 + dc
        ref = den_all.at[dy, lax.rem(z + NZ - dz_, NZ) * 2 + lax.rem(c + dc, 2)]
        return copy(ref, ref, d_send.at[i], d_recv.at[i], (blk, grp))

    docp = copy(den_mine.at[0], den_o, y_send.at[2], y_recv.at[2], ynb)
    for dz_ in (4, 3, 5, 2, 6, 1, 7, 0):
        if dz_ == 2:
            go(docp)
            go(d_copy(0, 1, 0))
        for dy in (0, 1):
            for dc in (0, 1):
                if dz_ or dc:
                    go(d_copy(dz_, dy, dc))

    psum = jnp.broadcast_to(jnp.sum(pos_s[...], axis=1, keepdims=True), (2 * ROWS, 128)).T
    pos_y[...] = psum[:1, ROWS:]
    pcp = copy(pos_y, pos_x, y_send.at[3], y_recv.at[3], ynb)
    go(pcp)
    pos_ref[...] = psum[:1, :ROWS]
    other_z(1)

    docp.wait_recv()
    d_arrived(0, 1, 0).wait_recv()
    me2 = z * 2 + c
    den_own = den_all[0, me2] + den_all[1, me2]
    lse_ref[...] = jnp.log(den_own)
    r_rows = 1.0 / jnp.concatenate([column(den_own), column(den_o[...] + den_mine[1])], axis=0)
    for n, dz_ in enumerate((0, 1, 7, 2, 6, 3, 5, 4)):
        for dy in (0, 1):
            for dc in (0, 1):
                if dz_ or dc:
                    d_arrived(dz_, dy, dc).wait_recv()
        zo = lax.rem(z + NZ - dz_, NZ)
        parts = []
        for k in range(2):
            r_cols = 1.0 / (den_all[0, zo * 2 + k] + den_all[1, zo * 2 + k])
            e = e_all[zo, :, k * ROWS : (k + 1) * ROWS]
            h = e * (r_rows + r_cols) - jnp.where(cols_of(zo, k) == pcol_s[...], 2.0, 0.0)
            parts.append(h.astype(BF16))
        g = jnp.dot(
            jnp.concatenate(parts, axis=1), ub_all[zo], preferred_element_type=F32
        )
        if n == 0:
            acc_s[...] = g
        else:
            acc_s[...] += g

    def other_half(q):
        cols = pl.ds(pl.multiple_of(c * half + q * cut, cut), cut)
        f_t[q * cut : (q + 1) * cut, ROWS : 2 * ROWS] = feat_o[:, cols].T

    other_z(2)
    other_z(3)
    for q in (0, 1):
        go(fc_copy(q))
    zo_ = u_s[ROWS:]
    inv_o = lax.rsqrt(jnp.sum(zo_ * zo_, axis=1, keepdims=True) + 1e-06)
    u_s[ROWS:] = zo_ * inv_o
    inv_s[ROWS:] = inv_o

    slope = acc_s[...] * INV_TEMP
    u = u_s[...]
    dz = inv_s[...] * (slope - u * jnp.sum(u * slope, axis=1, keepdims=True))
    dz_ref[...] = dz[:ROWS]
    hi = dz.astype(BF16)
    dzh[:2] = hi.reshape(2, ROWS, PROJ)
    xcp = copy(dzh.at[pl.ds(0, 2)], dzh.at[pl.ds(2, 2)], x_send.at[1], x_recv.at[1], sib)
    go(xcp)
    if LOW:
        dzl[:2] = (dz - hi.astype(F32)).astype(BF16).reshape(2, ROWS, PROJ)
        lcp = copy(dzl.at[pl.ds(0, 2)], dzl.at[pl.ds(2, 2)], x_send.at[2], x_recv.at[2], sib)
        go(lcp)
    for q in (0, 1):
        other_half(q)
        fc_copy(q).wait_recv()
        f_t[q * cut : (q + 1) * cut, 3 * ROWS :] = f_sib[1, :, q * cut : (q + 1) * cut].T
    xcp.wait_recv()
    if LOW:
        lcp.wait_recv()
    pl.semaphore_wait(in_sem, 4)
    ycp = copy(dzh.at[1], dzx, y_send.at[4], y_recv.at[4], ynb)

    def along(t, first, d):
        if (t % 2 == 0) == first:
            return dev(z, y, c, lax.rem(x + d, 4))
        return dev(z, lax.rem(y + d, 4), c, x)

    def place(t, first):
        return x if (t % 2 == 0) == first else y

    def s1_copy(t, d):
        j = lax.rem(place(t, True) + d, 4)
        return copy(sb1.at[t, j], r1.at[t, d - 1], s1_send.at[t, d - 1], s1_recv.at[t, d - 1], along(t, True, d))

    def s2_copy(t, d):
        j = lax.rem(place(t, False) + d, 4)
        return copy(qf.at[t, j], r2.at[t, d - 1], s2_send.at[t, d - 1], s2_recv.at[t, d - 1], along(t, False, d))

    def out_rows(t, a, b, n):
        start = c * (HID // 2) + t * 256 + a * 64 + b * 16
        return pl.ds(pl.multiple_of(start, 16), n)

    def zcols(j):
        return pl.ds(pl.multiple_of(lax.rem(j, 2) * 256, 256), 256)

    def zpeer(d):
        return dev(lax.rem(z + d, NZ), y, c, x)

    def s3_copy(d):
        j = lax.rem(z + d, NZ)
        return copy(zb.at[j // 2, :, zcols(j)], r3.at[d - 1], s3_send.at[d - 1], s3_recv.at[d - 1], zpeer(d))

    def zrows(j):
        t = j // 2
        odd = lax.rem(t, 2)
        return out_rows(t, x + odd * (y - x), y + odd * (x - y), 16)

    def g3_copy(d, mine_=True):
        j = z if mine_ else lax.rem(z + NZ - d, NZ)
        ref = head_ref.at[zrows(j), zcols(j)]
        return copy(ref, ref, g3_send.at[d - 1], g3_recv.at[d - 1], zpeer(d))

    def g2_copy(t, d, mine_=True):
        b = place(t, False)
        ref = head_ref.at[out_rows(t, place(t, True), b if mine_ else lax.rem(b + 4 - d, 4), 16), :]
        return copy(ref, ref, g2_send.at[t, d - 1], g2_recv.at[t, d - 1], along(t, False, d))

    def g1_copy(t, d, mine_=True):
        a = place(t, True)
        ref = head_ref.at[out_rows(t, a if mine_ else lax.rem(a + 4 - d, 4), 0, 64), :]
        return copy(ref, ref, g1_send.at[t, d - 1], g1_recv.at[t, d - 1], along(t, True, d))

    def gc_copy(t, d):
        a = place(t, True)
        ref = head_ref.at[out_rows(t, lax.rem(a + 4 - d, 4), 0, 64), :]
        return copy(ref, ref, gc_send.at[t, d], gc_recv.at[t, d], sib)

    def gc_arrived(t, d):
        start = (1 - c) * (HID // 2) + t * 256 + lax.rem(place(t, True) + 4 - d, 4) * 64
        ref = head_ref.at[pl.ds(pl.multiple_of(start, 64), 64), :]
        return copy(ref, ref, gc_send.at[t, d], gc_recv.at[t, d], sib)

    D3, D7 = (2, 1, 3), (4, 3, 5, 2, 6, 1, 7)

    def stage1(t):
        ft = f_t[t * 256 : (t + 1) * 256, :]
        part = jnp.dot(ft, dzh[...].reshape(4 * ROWS, PROJ), preferred_element_type=F32)
        if LOW:
            part += jnp.dot(ft, dzl[...].reshape(4 * ROWS, PROJ), preferred_element_type=F32)
        pf[t] = part.reshape(4, 64, PROJ)
        sb1[t] = part.astype(BF16).reshape(4, 64, PROJ)
        for d in D3:
            go(s1_copy(t, d))

    def stage2(t):
        for d in D3:
            s1_copy(t, d).wait_recv()
        total = pf[t, place(t, True)]
        for d in range(3):
            total = total + r1[t, d].astype(F32)
        qf[t] = total.reshape(4, 16, PROJ)
        for d in D3:
            go(s2_copy(t, d))

    def stage3():
        for t in range(4):
            for d in D3:
                s2_copy(t, d).wait_recv()
            zb[t] = qf[t, place(t, False)] + r2[t, 0] + r2[t, 1] + r2[t, 2]
        for d in D7:
            go(s3_copy(d))

    def stage4():
        total = zb[z // 2, :, zcols(z)]
        for d in D7:
            s3_copy(d).wait_recv()
        for d in range(7):
            total = total + r3[d]
        head_ref[zrows(z), zcols(z)] = total.astype(BF16)
        for d in D7:
            go(g3_copy(d))

    def stage5():
        for d in D7:
            g3_copy(d, False).wait_recv()
        for t in range(4):
            for d in D3:
                go(g2_copy(t, d))

    def stage6(t):
        for d in D3:
            g2_copy(t, d, False).wait_recv()
        for d in D3:
            go(g1_copy(t, d))
        go(gc_copy(t, 0))

    def stage7(t):
        for d in D3:
            g1_copy(t, d, False).wait_recv()
            go(gc_copy(t, d))

    for t in range(4):
        stage1(t)
    for t in range(4):
        stage2(t)
    stage3()
    go(ycp)
    flush()
    stage4()
    stage5()
    flush()
    for t in range(4):
        stage6(t)
    ycp.wait_recv()
    dz_ref[...] += dzx[...].astype(F32)
    pcp.wait_recv()
    pos_ref[...] = (pos_ref[...] + pos_x[...]) * INV_TEMP
    for t in range(4):
        stage7(t)
    for t in range(4):
        for d in range(4):
            gc_arrived(t, d).wait_recv()
    flush()


def finish(pos_in, lse_in, dz_in, head_in, pos_ref, lse_ref, dz_ref, head_ref, buf, sem):
    copies = [
        pltpu.make_async_copy(dz_in, dz_ref, sem.at[0]),
        pltpu.make_async_copy(pos_in, pos_ref, sem.at[1]),
        pltpu.make_async_copy(lse_in, lse_ref, sem.at[2]),
    ]
    for cp in copies:
        cp.start()
    for i in range(8):
        rows = slice(i * 256, (i + 1) * 256)
        buf[rows, :] = head_in[rows, :].astype(F32)
        cp = pltpu.make_async_copy(buf.at[rows, :], head_ref.at[rows, :], sem.at[3 + i])
        cp.start()
        copies.append(cp)
    for cp in copies:
        cp.wait()


def on_device(features, head_weight, pairs):
    vmem = pl.BlockSpec(memory_space=pltpu.VMEM)
    dma = pltpu.SemaphoreType.DMA
    pos, lse, dz, head = pl.pallas_call(
        kernel,
        out_shape=(
            pltpu.VMEM((1, ROWS), F32),
            pltpu.VMEM((1, ROWS), F32),
            pltpu.VMEM((ROWS, PROJ), F32),
            pltpu.VMEM((HID, PROJ), BF16),
        ),
        in_specs=[pl.BlockSpec(memory_space=pltpu.HBM)] * 3,
        out_specs=(vmem,) * 4,
        scratch_shapes=[
            pltpu.VMEM((ROWS, HID), BF16),
            pltpu.VMEM((HID, PROJ), BF16),
            pltpu.VMEM((1, ROWS), jnp.int32),
            dma((2 * KCUTS + 1,)),
            pltpu.VMEM((NZ, 2 * ROWS, PROJ), BF16),
            pltpu.VMEM((2, ROWS, PROJ), BF16),
            pltpu.VMEM((NZ, 2 * ROWS, 2 * ROWS), F32),
            pltpu.VMEM((2 * ROWS, PROJ), F32),
            pltpu.VMEM((2 * ROWS, 1), F32),
            pltpu.VMEM((2 * ROWS, 1), jnp.int32),
            pltpu.VMEM((2 * ROWS, 128), F32),
            pltpu.VMEM((2 * ROWS, 128), F32),
            pltpu.VMEM((2, 1, ROWS), F32),
            pltpu.VMEM((2, 2 * NZ, 1, ROWS), F32),
            pltpu.VMEM((1, ROWS), F32),
            pltpu.VMEM((1, ROWS), F32),
            pltpu.VMEM((1, ROWS), F32),
            pltpu.VMEM((2 * ROWS, PROJ), F32),
            pltpu.VMEM((ROWS, HID), BF16),
            pltpu.VMEM((1, ROWS), jnp.int32),
            pltpu.VMEM((2, ROWS, HID // 2), BF16),
            pltpu.VMEM((HID // 2, 4 * ROWS), BF16),
            pltpu.VMEM((4, ROWS, PROJ), BF16),
            pltpu.VMEM((4, ROWS, PROJ), BF16),
            pltpu.VMEM((ROWS, PROJ), BF16),
            pltpu.VMEM((4, 4, 64, PROJ), F32),
            pltpu.VMEM((4, 4, 64, PROJ), BF16),
            pltpu.VMEM((4, 3, 64, PROJ), BF16),
            pltpu.VMEM((4, 4, 16, PROJ), F32),
            pltpu.VMEM((4, 3, 16, PROJ), F32),
            pltpu.VMEM((4, 16, PROJ), F32),
            pltpu.VMEM((7, 16, 256), F32),
            pltpu.SemaphoreType.REGULAR,
            dma((2, 4, 4)), dma((2, 4, 4)),
            dma((5,)), dma((5,)),
            dma((KCUTS,)), dma((KCUTS,)),
            dma((2, 5)), dma((2, 5)),
            dma((2,)), dma((2,)),
            dma((32,)), dma((32,)),
            dma((3,)), dma((3,)),
            dma((4, 3)), dma((4, 3)),
            dma((4, 3)), dma((4, 3)),
            dma((7,)), dma((7,)),
            dma((7,)), dma((7,)),
            dma((4, 3)), dma((4, 3)),
            dma((4, 3)), dma((4, 3)),
            dma((4, 4)), dma((4, 4)),
        ],
        compiler_params=pltpu.CompilerParams(
            collective_id=0, has_side_effects=True, vmem_limit_bytes=44 << 20
        ),
        name="ntxent",
    )(*[pltpu.with_memory_space_constraint(a, pltpu.HBM) for a in (features[0], head_weight, pairs)])
    inputs = [pltpu.with_memory_space_constraint(a, pltpu.VMEM) for a in (pos, lse, dz, head)]
    pos, lse, dz, head = pl.pallas_call(
        finish,
        out_shape=(
            jax.ShapeDtypeStruct((1, ROWS), F32),
            jax.ShapeDtypeStruct((1, ROWS), F32),
            jax.ShapeDtypeStruct((ROWS, PROJ), F32),
            jax.ShapeDtypeStruct((HID, PROJ), F32),
        ),
        in_specs=[vmem] * 4,
        out_specs=(pl.BlockSpec(memory_space=pl.ANY),) * 4,
        scratch_shapes=[pltpu.VMEM((HID, PROJ), F32), dma((11,))],
        compiler_params=pltpu.CompilerParams(vmem_limit_bytes=16 << 20),
        name="finish",
    )(*inputs)
    return pos, lse, dz[None], head


def solution(mesh):
    in_specs = (P("group", "blk", None), P(), P("group", "blk"))
    out_specs = (P("group", "blk"), P("group", "blk"), P("group", "blk", None), P())
    return jax.shard_map(
        on_device, mesh=mesh, in_specs=in_specs, out_specs=out_specs, check_vma=False
    )
```

```python
import functools

import jax
import jax.numpy as jnp
from jax import lax
from jax.experimental import pallas as pl
from jax.experimental.pallas import tpu as pltpu
from jax.sharding import PartitionSpec as P

MESH = pl.DeviceIdType.MESH
F32 = jnp.float32
BF16 = jnp.bfloat16

HID = 2048
PROJ = 512
ROWS = 256
NZ = 8
CUT = 64
KCUTS = 4
INV_TEMP = 10.0
LOG2E = 1.4426950408889634


def kernel(
    feat_hbm, w_hbm, pairs_hbm,
    pos_ref, lse_ref, dz_ref, head_ref,
    feat_ref, w_ref, pairs_ref, load_sem,
    ub_all, ub_r, e_all, u_s, inv_s, pcol_s, den_s, pos_s, den_mine, den_all, den_o, pos_x, pos_y,
    acc_s, feat_o, pairs_o, f_sib, f_t, dzh, dzl, dzx, pf, sb1, r1, qf, r2, zb, r3, in_sem,
    z_send, z_recv, y_send, y_recv, fy_send, fy_recv, c_send, c_recv, fc_send, fc_recv,
    d_send, d_recv, x_send, x_recv, s1_send, s1_recv, s2_send, s2_recv, s3_send, s3_recv,
    g3_send, g3_recv, g2_send, g2_recv, g1_send, g1_recv, gc_send, gc_recv,
):
    blk = lax.axis_index("blk")
    grp = lax.axis_index("group")
    z, yl, c = blk // 4, lax.rem(blk // 2, 2), lax.rem(blk, 2)
    yh, x = grp // 4, lax.rem(grp, 4)
    y = yh * 2 + yl

    def dev(z_, y_, c_, x_):
        return ((z_ * 2 + lax.rem(y_, 2)) * 2 + c_, (y_ // 2) * 4 + x_)

    def copy(src, dst, ssem, rsem, to):
        return pltpu.make_async_remote_copy(
            src_ref=src, dst_ref=dst, send_sem=ssem, recv_sem=rsem,
            device_id=to, device_id_type=MESH,
        )

    sib = dev(z, y, 1 - c, x)
    ynb = (blk + 2 - 4 * yl, grp)

    barrier = pltpu.get_barrier_semaphore()
    ring = (
        dev(z, y, c, lax.rem(x + 1, 4)),
        dev(z, y, c, lax.rem(x + 3, 4)),
        dev(z, lax.rem(y + 1, 4), c, x),
        dev(z, lax.rem(y + 3, 4), c, x),
    )
    znext = (dev(lax.rem(z + 1, NZ), y, c, x), dev(lax.rem(z + NZ - 1, NZ), y, c, x))
    for to in znext + (sib,) + ring:
        pl.semaphore_signal(barrier, inc=1, device_id=to, device_id_type=MESH)

    def kcut(k):
        return slice(k * (HID // KCUTS), (k + 1) * (HID // KCUTS))

    loads = []
    for k in range(KCUTS):
        loads.append(pltpu.make_async_copy(feat_hbm.at[:, kcut(k)], feat_ref.at[:, kcut(k)], load_sem.at[2 * k]))
        loads.append(pltpu.make_async_copy(w_hbm.at[kcut(k), :], w_ref.at[kcut(k), :], load_sem.at[2 * k + 1]))
    loads.append(pltpu.make_async_copy(pairs_hbm, pairs_ref, load_sem.at[2 * KCUTS]))
    for cp in loads:
        cp.start()

    zz = jnp.zeros((ROWS, PROJ), F32)
    for k in range(KCUTS):
        for cp in loads[2 * k : 2 * k + 2]:
            cp.wait()
        zz += jnp.dot(feat_ref[:, kcut(k)], w_ref[kcut(k), :], preferred_element_type=F32)
    loads[-1].wait()
    inv = lax.rsqrt(jnp.sum(zz * zz, axis=1, keepdims=True) + 1e-06)
    u = zz * inv
    inv_s[:ROWS] = inv
    u_s[:ROWS] = u
    ub = u.astype(BF16)
    ub_r[0] = ub
    ub_all[z, pl.ds(pl.multiple_of(c * ROWS, ROWS), ROWS), :] = ub
    pl.semaphore_wait(barrier, 7)

    def origin(dr, s):
        return lax.rem(z + NZ + (-s if dr == 0 else s), NZ)

    def piece(zo, c_, off, n):
        return ub_all.at[zo, pl.ds(pl.multiple_of(c_ * ROWS + off, 16), n), :]

    def z_copy(dr, s, p):
        ref = piece(origin(dr, s), c, p * CUT, CUT)
        return copy(ref, ref, z_send.at[dr, s, p], z_recv.at[dr, s, p], znext[dr])

    def z_arrived(dr, s, p):
        ref = piece(origin(dr, s + 1), c, p * CUT, CUT)
        return copy(ref, ref, z_send.at[dr, s, p], z_recv.at[dr, s, p], znext[dr])

    def c_ref(dr, s, c_):
        return piece(origin(dr, s), c_, *((dr * 128, 128) if s == 4 else (0, ROWS)))

    def c_copy(dr, s):
        ref = c_ref(dr, s, c)
        return copy(ref, ref, c_send.at[dr, s], c_recv.at[dr, s], sib)

    def c_arrived(dr, s):
        ref = c_ref(dr, s, 1 - c)
        return copy(ref, ref, c_send.at[dr, s], c_recv.at[dr, s], sib)

    sent = []

    def go(cp):
        cp.start()
        sent.append(cp)

    def flush():
        for cp in sent:
            cp.wait_send()
        sent.clear()

    yub = copy(ub_r.at[0], ub_r.at[1], y_send.at[0], y_recv.at[0], ynb)
    ypairs = copy(pairs_ref, pairs_o, y_send.at[1], y_recv.at[1], ynb)
    go(yub)
    go(ypairs)
    for p in range(4):
        for dr in (0, 1):
            go(z_copy(dr, 0, p))
    go(c_copy(0, 0))

    def fy_copy(k):
        return copy(feat_ref.at[:, kcut(k)], feat_o.at[:, kcut(k)], fy_send.at[k], fy_recv.at[k], ynb)

    for k in range(KCUTS):
        go(fy_copy(k))
    for to in ring:
        pl.semaphore_signal(in_sem, inc=1, device_id=to, device_id_type=MESH)

    half = HID // 2
    cut = HID // KCUTS
    mine = pl.multiple_of(c * half, half)
    theirs = pl.multiple_of((1 - c) * half, half)
    xcp = copy(feat_ref.at[:, pl.ds(theirs, half)], f_sib.at[0], x_send.at[0], x_recv.at[0], sib)
    go(xcp)

    def fc_copy(q):
        cols = pl.ds(pl.multiple_of((1 - c) * half + q * cut, cut), cut)
        dst = f_sib.at[1, :, q * cut : (q + 1) * cut]
        return copy(feat_o.at[:, cols], dst, fc_send.at[q], fc_recv.at[q], sib)

    den_s[...] = jnp.zeros_like(den_s)
    pos_s[...] = jnp.zeros_like(pos_s)
    sub = lax.broadcasted_iota(jnp.int32, (2 * ROWS, 1), 0)
    other_blk = blk + 2 - 4 * yl
    own_row = jnp.where(sub < ROWS, blk * ROWS, other_blk * ROWS - ROWS) + sub

    def column(row):
        return jnp.broadcast_to(row, (128, ROWS)).T[:, :1]

    def cols_of(zo, k):
        first = (zo * 4 + yl * 2 + k) * ROWS
        return first + lax.broadcasted_iota(jnp.int32, (2 * ROWS, ROWS), 1)

    def scores(zo, k):
        lanes = pl.ds(pl.multiple_of(k * ROWS, ROWS), ROWS)
        s = lax.dot_general(
            ub_r[...].reshape(2 * ROWS, PROJ), ub_all[zo, lanes, :],
            (((1,), (1,)), ((), ())), preferred_element_type=F32,
        )
        cols = cols_of(zo, k)
        e = jnp.where(cols == own_row, 0.0, jnp.exp2(s * (INV_TEMP * LOG2E)))
        e_all[zo, :, lanes] = e
        p = jnp.where(cols == pcol_s[...], s, 0.0)
        den_s[...] += e[:, :128] + e[:, 128:]
        pos_s[...] += p[:, :128] + p[:, 128:]

    def other_z(k):
        fy_copy(k).wait_recv()
        part = jnp.dot(feat_o[:, kcut(k)], w_ref[kcut(k), :], preferred_element_type=F32)
        if k == 0:
            u_s[ROWS:] = part
        else:
            u_s[ROWS:] += part

    for s in (1, 2, 3):
        for p in range(4):
            for dr in (0, 1):
                z_arrived(dr, s - 1, p).wait_recv()
                if s < 3 or p // 2 == dr:
                    go(z_copy(dr, s, p))
                if p == 3:
                    go(c_copy(dr, s))
            if s == 1:
                if p == 1:
                    f_t[:, :ROWS] = feat_ref[:, pl.ds(mine, half)].T
                if p == 2:
                    xcp.wait_recv()
                    f_t[:, 2 * ROWS : 3 * ROWS] = f_sib[0].T
                if p == 3:
                    yub.wait_recv()
                    ypairs.wait_recv()
                    pcol_s[:ROWS] = column(pairs_ref[...])
                    pcol_s[ROWS:] = column(pairs_o[...])
                    scores(z, c)
                    c_arrived(0, 0).wait_recv()
                    scores(z, 1 - c)
            else:
                dr = p % 2
                if p >= 2:
                    c_arrived(dr, s - 1).wait_recv()
                scores(origin(dr, s - 1), c if p < 2 else 1 - c)
    for dr in (0, 1):
        scores(origin(dr, 3), c)
    other_z(0)
    for dr in (0, 1):
        c_arrived(dr, 3).wait_recv()
        scores(origin(dr, 3), 1 - c)
    far = origin(0, 4)
    for dr in (0, 1):
        for p in (2 * dr, 2 * dr + 1):
            z_arrived(dr, 3, p).wait_recv()
        go(c_copy(dr, 4))
    scores(far, c)
    for dr in (0, 1):
        c_arrived(dr, 4).wait_recv()
    scores(far, 1 - c)

    sums = jnp.sum(den_s[...].T, axis=0, keepdims=True)
    den_mine[0] = sums[:, :ROWS]
    den_mine[1] = sums[:, ROWS:]
    den_all[0, z * 2 + c] = sums[:, :ROWS]

    def d_copy(dz_, dy, dc):
        to_blk = lax.rem(z + dz_, NZ) * 4 + lax.rem(yl + dy, 2) * 2 + lax.rem(c + dc, 2)
        i = dz_ * 4 + dy * 2 + dc
        return copy(
            den_mine.at[dy], den_all.at[dy, z * 2 + c], d_send.at[i], d_recv.at[i], (to_blk, grp)
        )

    def d_arrived(dz_, dy, dc):
        i = dz_ * 4 + dy * 2 + dc
        ref = den_all.at[dy, lax.rem(z + NZ - dz_, NZ) * 2 + lax.rem(c + dc, 2)]
        return copy(ref, ref, d_send.at[i], d_recv.at[i], (blk, grp))

    docp = copy(den_mine.at[0], den_o, y_send.at[2], y_recv.at[2], ynb)
    for dz_ in (4, 3, 5, 2, 6, 1, 7, 0):
        if dz_ == 2:
            go(docp)
            go(d_copy(0, 1, 0))
        for dy in (0, 1):
            for dc in (0, 1):
                if dz_ or dc:
                    go(d_copy(dz_, dy, dc))

    psum = jnp.sum(pos_s[...].T, axis=0, keepdims=True)
    pos_y[...] = psum[:1, ROWS:]
    pcp = copy(pos_y, pos_x, y_send.at[3], y_recv.at[3], ynb)
    go(pcp)
    pos_ref[...] = psum[:1, :ROWS]
    other_z(1)
    other_z(2)

    def other_half(q):
        cols = pl.ds(pl.multiple_of(c * half + q * cut, cut), cut)
        f_t[q * cut : (q + 1) * cut, ROWS : 2 * ROWS] = feat_o[:, cols].T

    def other_rest():
        other_z(3)
        for q in (0, 1):
            go(fc_copy(q))
        zo_ = u_s[ROWS:]
        inv_o = lax.rsqrt(jnp.sum(zo_ * zo_, axis=1, keepdims=True) + 1e-06)
        u_s[ROWS:] = zo_ * inv_o
        inv_s[ROWS:] = inv_o

    def other_from_sib(q):
        fc_copy(q).wait_recv()
        f_t[q * cut : (q + 1) * cut, 3 * ROWS :] = f_sib[1, :, q * cut : (q + 1) * cut].T

    docp.wait_recv()
    d_arrived(0, 1, 0).wait_recv()
    me2 = z * 2 + c
    den_own = den_all[0, me2] + den_all[1, me2]
    lse_ref[...] = jnp.log(den_own)
    r_rows = 1.0 / jnp.concatenate([column(den_own), column(den_o[...] + den_mine[1])], axis=0)
    for n, dz_ in enumerate((0, 1, 7, 2, 6, 3, 5, 4)):
        for dy in (0, 1):
            for dc in (0, 1):
                if dz_ or dc:
                    d_arrived(dz_, dy, dc).wait_recv()
        zo = lax.rem(z + NZ - dz_, NZ)
        parts = []
        for k in range(2):
            r_cols = 1.0 / (den_all[0, zo * 2 + k] + den_all[1, zo * 2 + k])
            e = e_all[zo, :, k * ROWS : (k + 1) * ROWS]
            h = e * (r_rows + r_cols) - jnp.where(cols_of(zo, k) == pcol_s[...], 2.0, 0.0)
            parts.append(h.astype(BF16))
        g = jnp.dot(
            jnp.concatenate(parts, axis=1), ub_all[zo], preferred_element_type=F32
        )
        if n == 0:
            acc_s[...] = g
            other_rest()
        else:
            acc_s[...] += g
        if n in (1, 2):
            other_half(n - 1)
        if n in (4, 5):
            other_from_sib(n - 4)

    slope = acc_s[...] * INV_TEMP
    u = u_s[...]
    dz = inv_s[...] * (slope - u * jnp.sum(u * slope, axis=1, keepdims=True))
    dz_ref[...] = dz[:ROWS]
    hi = dz.astype(BF16)
    lo = (dz - hi.astype(F32)).astype(BF16)
    dzh[:2] = hi.reshape(2, ROWS, PROJ)
    xcp = copy(dzh.at[pl.ds(0, 2)], dzh.at[pl.ds(2, 2)], x_send.at[1], x_recv.at[1], sib)
    go(xcp)
    dzl[:2] = lo.reshape(2, ROWS, PROJ)
    lcp = copy(dzl.at[pl.ds(0, 2)], dzl.at[pl.ds(2, 2)], x_send.at[2], x_recv.at[2], sib)

    for t in range(4):
        ft = f_t[t * 256 : (t + 1) * 256, : 2 * ROWS]
        part = jnp.dot(ft, hi, preferred_element_type=F32)
        part += jnp.dot(ft, lo, preferred_element_type=F32)
        pf[t] = part.reshape(4, 64, PROJ)
        if t == 2:
            go(lcp)
    xcp.wait_recv()
    pl.semaphore_wait(in_sem, 4)
    ycp = copy(dzh.at[1], dzx, y_send.at[4], y_recv.at[4], ynb)

    def along(t, first, d):
        if (t % 2 == 0) == first:
            return dev(z, y, c, lax.rem(x + d, 4))
        return dev(z, lax.rem(y + d, 4), c, x)

    def place(t, first):
        return x if (t % 2 == 0) == first else y

    def s1_copy(t, d):
        j = lax.rem(place(t, True) + d, 4)
        return copy(sb1.at[t, j], r1.at[t, d - 1], s1_send.at[t, d - 1], s1_recv.at[t, d - 1], along(t, True, d))

    def s2_copy(t, d):
        j = lax.rem(place(t, False) + d, 4)
        return copy(qf.at[t, j], r2.at[t, d - 1], s2_send.at[t, d - 1], s2_recv.at[t, d - 1], along(t, False, d))

    def out_rows(t, a, b, n):
        start = c * (HID // 2) + t * 256 + a * 64 + b * 16
        return pl.ds(pl.multiple_of(start, 16), n)

    def zcols(j):
        return pl.ds(pl.multiple_of(lax.rem(j, 2) * 256, 256), 256)

    def zpeer(d):
        return dev(lax.rem(z + d, NZ), y, c, x)

    def s3_copy(d):
        j = lax.rem(z + d, NZ)
        return copy(zb.at[j // 2, :, zcols(j)], r3.at[d - 1], s3_send.at[d - 1], s3_recv.at[d - 1], zpeer(d))

    def zrows(j):
        t = j // 2
        odd = lax.rem(t, 2)
        return out_rows(t, x + odd * (y - x), y + odd * (x - y), 16)

    def g3_copy(d, mine_=True):
        j = z if mine_ else lax.rem(z + NZ - d, NZ)
        ref = head_ref.at[zrows(j), zcols(j)]
        return copy(ref, ref, g3_send.at[d - 1], g3_recv.at[d - 1], zpeer(d))

    def g2_copy(t, d, mine_=True):
        b = place(t, False)
        ref = head_ref.at[out_rows(t, place(t, True), b if mine_ else lax.rem(b + 4 - d, 4), 16), :]
        return copy(ref, ref, g2_send.at[t, d - 1], g2_recv.at[t, d - 1], along(t, False, d))

    def g1_copy(t, d, mine_=True):
        a = place(t, True)
        ref = head_ref.at[out_rows(t, a if mine_ else lax.rem(a + 4 - d, 4), 0, 64), :]
        return copy(ref, ref, g1_send.at[t, d - 1], g1_recv.at[t, d - 1], along(t, True, d))

    def gc_copy(t, d):
        a = place(t, True)
        ref = head_ref.at[out_rows(t, lax.rem(a + 4 - d, 4), 0, 64), :]
        return copy(ref, ref, gc_send.at[t, d], gc_recv.at[t, d], sib)

    def gc_arrived(t, d):
        start = (1 - c) * (HID // 2) + t * 256 + lax.rem(place(t, True) + 4 - d, 4) * 64
        ref = head_ref.at[pl.ds(pl.multiple_of(start, 64), 64), :]
        return copy(ref, ref, gc_send.at[t, d], gc_recv.at[t, d], sib)

    D3, D7 = (2, 1, 3), (4, 3, 5, 2, 6, 1, 7)

    def stage1(t):
        ft = f_t[t * 256 : (t + 1) * 256, 2 * ROWS :]
        part = pf[t].reshape(256, PROJ)
        for low in (False, True):
            if low and t == 2:
                lcp.wait_recv()
            if low and t < 2:
                continue
            d = (dzl if low else dzh)[2:].reshape(2 * ROWS, PROJ)
            part = part + jnp.dot(ft, d, preferred_element_type=F32)
        pf[t] = part.reshape(4, 64, PROJ)
        sb1[t] = part.astype(BF16).reshape(4, 64, PROJ)
        for d in D3:
            go(s1_copy(t, d))

    def stage2(t):
        for d in D3:
            s1_copy(t, d).wait_recv()
        total = pf[t, place(t, True)]
        for d in range(3):
            total = total + r1[t, d].astype(F32)
        qf[t] = total.reshape(4, 16, PROJ)
        for d in D3:
            go(s2_copy(t, d))

    def stage3():
        for t in range(4):
            for d in D3:
                s2_copy(t, d).wait_recv()
            zb[t] = qf[t, place(t, False)] + r2[t, 0] + r2[t, 1] + r2[t, 2]
        for d in D7:
            go(s3_copy(d))

    def stage4():
        total = zb[z // 2, :, zcols(z)]
        for d in D7:
            s3_copy(d).wait_recv()
        for d in range(7):
            total = total + r3[d]
        head_ref[zrows(z), zcols(z)] = total.astype(BF16)
        for d in D7:
            go(g3_copy(d))

    def stage5():
        for d in D7:
            g3_copy(d, False).wait_recv()
        for t in range(4):
            for d in D3:
                go(g2_copy(t, d))

    def stage6(t):
        for d in D3:
            g2_copy(t, d, False).wait_recv()
        for d in D3:
            go(g1_copy(t, d))
        go(gc_copy(t, 0))

    def stage7(t):
        for d in D3:
            g1_copy(t, d, False).wait_recv()
            go(gc_copy(t, d))

    for t in range(4):
        stage1(t)
    for t in range(4):
        stage2(t)
    stage3()
    go(ycp)
    flush()
    stage4()
    stage5()
    flush()
    for t in range(4):
        stage6(t)
    ycp.wait_recv()
    dz_ref[...] += dzx[...].astype(F32)
    pcp.wait_recv()
    pos_ref[...] = (pos_ref[...] + pos_x[...]) * INV_TEMP
    for t in range(4):
        stage7(t)
    for t in range(4):
        for d in range(4):
            gc_arrived(t, d).wait_recv()
    flush()


def finish(pos_in, lse_in, dz_in, head_in, pos_ref, lse_ref, dz_ref, head_ref, buf, sem):
    copies = [
        pltpu.make_async_copy(dz_in, dz_ref, sem.at[0]),
        pltpu.make_async_copy(pos_in, pos_ref, sem.at[1]),
        pltpu.make_async_copy(lse_in, lse_ref, sem.at[2]),
    ]
    for cp in copies:
        cp.start()
    for i in range(8):
        rows = slice(i * 256, (i + 1) * 256)
        buf[rows, :] = head_in[rows, :].astype(F32)
        cp = pltpu.make_async_copy(buf.at[rows, :], head_ref.at[rows, :], sem.at[3 + i])
        cp.start()
        copies.append(cp)
    for cp in copies:
        cp.wait()


def on_device(features, head_weight, pairs):
    vmem = pl.BlockSpec(memory_space=pltpu.VMEM)
    dma = pltpu.SemaphoreType.DMA
    pos, lse, dz, head = pl.pallas_call(
        kernel,
        out_shape=(
            pltpu.VMEM((1, ROWS), F32),
            pltpu.VMEM((1, ROWS), F32),
            pltpu.VMEM((ROWS, PROJ), F32),
            pltpu.VMEM((HID, PROJ), BF16),
        ),
        in_specs=[pl.BlockSpec(memory_space=pltpu.HBM)] * 3,
        out_specs=(vmem,) * 4,
        scratch_shapes=[
            pltpu.VMEM((ROWS, HID), BF16),
            pltpu.VMEM((HID, PROJ), BF16),
            pltpu.VMEM((1, ROWS), jnp.int32),
            dma((2 * KCUTS + 1,)),
            pltpu.VMEM((NZ, 2 * ROWS, PROJ), BF16),
            pltpu.VMEM((2, ROWS, PROJ), BF16),
            pltpu.VMEM((NZ, 2 * ROWS, 2 * ROWS), F32),
            pltpu.VMEM((2 * ROWS, PROJ), F32),
            pltpu.VMEM((2 * ROWS, 1), F32),
            pltpu.VMEM((2 * ROWS, 1), jnp.int32),
            pltpu.VMEM((2 * ROWS, 128), F32),
            pltpu.VMEM((2 * ROWS, 128), F32),
            pltpu.VMEM((2, 1, ROWS), F32),
            pltpu.VMEM((2, 2 * NZ, 1, ROWS), F32),
            pltpu.VMEM((1, ROWS), F32),
            pltpu.VMEM((1, ROWS), F32),
            pltpu.VMEM((1, ROWS), F32),
            pltpu.VMEM((2 * ROWS, PROJ), F32),
            pltpu.VMEM((ROWS, HID), BF16),
            pltpu.VMEM((1, ROWS), jnp.int32),
            pltpu.VMEM((2, ROWS, HID // 2), BF16),
            pltpu.VMEM((HID // 2, 4 * ROWS), BF16),
            pltpu.VMEM((4, ROWS, PROJ), BF16),
            pltpu.VMEM((4, ROWS, PROJ), BF16),
            pltpu.VMEM((ROWS, PROJ), BF16),
            pltpu.VMEM((4, 4, 64, PROJ), F32),
            pltpu.VMEM((4, 4, 64, PROJ), BF16),
            pltpu.VMEM((4, 3, 64, PROJ), BF16),
            pltpu.VMEM((4, 4, 16, PROJ), F32),
            pltpu.VMEM((4, 3, 16, PROJ), F32),
            pltpu.VMEM((4, 16, PROJ), F32),
            pltpu.VMEM((7, 16, 256), F32),
            pltpu.SemaphoreType.REGULAR,
            dma((2, 4, 4)), dma((2, 4, 4)),
            dma((5,)), dma((5,)),
            dma((KCUTS,)), dma((KCUTS,)),
            dma((2, 5)), dma((2, 5)),
            dma((2,)), dma((2,)),
            dma((32,)), dma((32,)),
            dma((3,)), dma((3,)),
            dma((4, 3)), dma((4, 3)),
            dma((4, 3)), dma((4, 3)),
            dma((7,)), dma((7,)),
            dma((7,)), dma((7,)),
            dma((4, 3)), dma((4, 3)),
            dma((4, 3)), dma((4, 3)),
            dma((4, 4)), dma((4, 4)),
        ],
        compiler_params=pltpu.CompilerParams(
            collective_id=0, has_side_effects=True, vmem_limit_bytes=44 << 20
        ),
        name="ntxent",
    )(*[pltpu.with_memory_space_constraint(a, pltpu.HBM) for a in (features[0], head_weight, pairs)])
    inputs = [pltpu.with_memory_space_constraint(a, pltpu.VMEM) for a in (pos, lse, dz, head)]
    pos, lse, dz, head = pl.pallas_call(
        finish,
        out_shape=(
            jax.ShapeDtypeStruct((1, ROWS), F32),
            jax.ShapeDtypeStruct((1, ROWS), F32),
            jax.ShapeDtypeStruct((ROWS, PROJ), F32),
            jax.ShapeDtypeStruct((HID, PROJ), F32),
        ),
        in_specs=[vmem] * 4,
        out_specs=(pl.BlockSpec(memory_space=pl.ANY),) * 4,
        scratch_shapes=[pltpu.VMEM((HID, PROJ), F32), dma((11,))],
        compiler_params=pltpu.CompilerParams(vmem_limit_bytes=16 << 20),
        name="finish",
    )(*inputs)
    return pos, lse, dz[None], head


def solution(mesh):
    in_specs = (P("group", "blk", None), P(), P("group", "blk"))
    out_specs = (P("group", "blk"), P("group", "blk"), P("group", "blk", None), P())
    return jax.shard_map(
        on_device, mesh=mesh, in_specs=in_specs, out_specs=out_specs, check_vma=False
    )
```

```python
import functools

import jax
import jax.numpy as jnp
from jax import lax
from jax.experimental import pallas as pl
from jax.experimental.pallas import tpu as pltpu
from jax.sharding import PartitionSpec as P

MESH = pl.DeviceIdType.MESH
F32 = jnp.float32
BF16 = jnp.bfloat16

HID = 2048
PROJ = 512
ROWS = 256
NZ = 8
CUT = 64
KCUTS = 4
INV_TEMP = 10.0
LOG2E = 1.4426950408889634


def kernel(
    feat_hbm, w_hbm, pairs_hbm,
    pos_ref, lse_ref, dz_ref, head_ref,
    feat_ref, w_ref, pairs_ref, load_sem,
    ub_all, ub_r, e_all, u_s, inv_s, pcol_s, r_s, den_s, pos_s, den_mine, den_all, den_o, pos_x, pos_y,
    acc_s, feat_o, pairs_o, f_sib, f_t, dzh, dzl, dzx, pf, sb1, r1, qf, r2, zb, r3, in_sem,
    z_send, z_recv, y_send, y_recv, fy_send, fy_recv, c_send, c_recv, fc_send, fc_recv,
    d_send, d_recv, x_send, x_recv, s1_send, s1_recv, s2_send, s2_recv, s3_send, s3_recv,
    g3_send, g3_recv, g2_send, g2_recv, g1_send, g1_recv, gc_send, gc_recv,
):
    blk = lax.axis_index("blk")
    grp = lax.axis_index("group")
    z, yl, c = blk // 4, lax.rem(blk // 2, 2), lax.rem(blk, 2)
    yh, x = grp // 4, lax.rem(grp, 4)
    y = yh * 2 + yl

    def dev(z_, y_, c_, x_):
        return ((z_ * 2 + lax.rem(y_, 2)) * 2 + c_, (y_ // 2) * 4 + x_)

    def copy(src, dst, ssem, rsem, to):
        return pltpu.make_async_remote_copy(
            src_ref=src, dst_ref=dst, send_sem=ssem, recv_sem=rsem,
            device_id=to, device_id_type=MESH,
        )

    sib = dev(z, y, 1 - c, x)
    ynb = (blk + 2 - 4 * yl, grp)

    barrier = pltpu.get_barrier_semaphore()
    ring = (
        dev(z, y, c, lax.rem(x + 1, 4)),
        dev(z, y, c, lax.rem(x + 3, 4)),
        dev(z, lax.rem(y + 1, 4), c, x),
        dev(z, lax.rem(y + 3, 4), c, x),
    )
    znext = (dev(lax.rem(z + 1, NZ), y, c, x), dev(lax.rem(z + NZ - 1, NZ), y, c, x))
    for to in znext + (sib,) + ring:
        pl.semaphore_signal(barrier, inc=1, device_id=to, device_id_type=MESH)

    def kcut(k):
        return slice(k * (HID // KCUTS), (k + 1) * (HID // KCUTS))

    loads = []
    for k in range(KCUTS):
        loads.append(pltpu.make_async_copy(feat_hbm.at[:, kcut(k)], feat_ref.at[:, kcut(k)], load_sem.at[2 * k]))
        loads.append(pltpu.make_async_copy(w_hbm.at[kcut(k), :], w_ref.at[kcut(k), :], load_sem.at[2 * k + 1]))
    loads.append(pltpu.make_async_copy(pairs_hbm, pairs_ref, load_sem.at[2 * KCUTS]))
    for cp in loads:
        cp.start()

    zz = jnp.zeros((ROWS, PROJ), F32)
    for k in range(KCUTS):
        for cp in loads[2 * k : 2 * k + 2]:
            cp.wait()
        zz += jnp.dot(feat_ref[:, kcut(k)], w_ref[kcut(k), :], preferred_element_type=F32)
    loads[-1].wait()
    inv = lax.rsqrt(jnp.sum(zz * zz, axis=1, keepdims=True) + 1e-06)
    u = zz * inv
    inv_s[:ROWS] = inv
    u_s[:ROWS] = u
    ub = u.astype(BF16)
    ub_r[0] = ub
    ub_all[z, pl.ds(pl.multiple_of(c * ROWS, ROWS), ROWS), :] = ub
    pl.semaphore_wait(barrier, 7)

    def origin(dr, s):
        return lax.rem(z + NZ + (-s if dr == 0 else s), NZ)

    def piece(zo, c_, off, n):
        return ub_all.at[zo, pl.ds(pl.multiple_of(c_ * ROWS + off, 16), n), :]

    def z_copy(dr, s, p):
        ref = piece(origin(dr, s), c, p * CUT, CUT)
        return copy(ref, ref, z_send.at[dr, s, p], z_recv.at[dr, s, p], znext[dr])

    def z_arrived(dr, s, p):
        ref = piece(origin(dr, s + 1), c, p * CUT, CUT)
        return copy(ref, ref, z_send.at[dr, s, p], z_recv.at[dr, s, p], znext[dr])

    def c_ref(dr, s, c_):
        return piece(origin(dr, s), c_, *((dr * 128, 128) if s == 4 else (0, ROWS)))

    def c_copy(dr, s):
        ref = c_ref(dr, s, c)
        return copy(ref, ref, c_send.at[dr, s], c_recv.at[dr, s], sib)

    def c_arrived(dr, s):
        ref = c_ref(dr, s, 1 - c)
        return copy(ref, ref, c_send.at[dr, s], c_recv.at[dr, s], sib)

    sent = []

    def go(cp):
        cp.start()
        sent.append(cp)

    def flush():
        for cp in sent:
            cp.wait_send()
        sent.clear()

    yub = copy(ub_r.at[0], ub_r.at[1], y_send.at[0], y_recv.at[0], ynb)
    ypairs = copy(pairs_ref, pairs_o, y_send.at[1], y_recv.at[1], ynb)
    go(yub)
    go(ypairs)
    for p in range(4):
        for dr in (0, 1):
            go(z_copy(dr, 0, p))
    go(c_copy(0, 0))

    def fy_copy(k):
        return copy(feat_ref.at[:, kcut(k)], feat_o.at[:, kcut(k)], fy_send.at[k], fy_recv.at[k], ynb)

    for k in range(KCUTS):
        go(fy_copy(k))
    for to in ring:
        pl.semaphore_signal(in_sem, inc=1, device_id=to, device_id_type=MESH)

    half = HID // 2
    cut = HID // KCUTS
    mine = pl.multiple_of(c * half, half)
    theirs = pl.multiple_of((1 - c) * half, half)
    xcp = copy(feat_ref.at[:, pl.ds(theirs, half)], f_sib.at[0], x_send.at[0], x_recv.at[0], sib)
    go(xcp)

    def fc_copy(q):
        cols = pl.ds(pl.multiple_of((1 - c) * half + q * cut, cut), cut)
        dst = f_sib.at[1, :, q * cut : (q + 1) * cut]
        return copy(feat_o.at[:, cols], dst, fc_send.at[q], fc_recv.at[q], sib)

    den_s[...] = jnp.zeros_like(den_s)
    pos_s[...] = jnp.zeros_like(pos_s)
    sub = lax.broadcasted_iota(jnp.int32, (2 * ROWS, 1), 0)
    other_blk = blk + 2 - 4 * yl
    own_row = jnp.where(sub < ROWS, blk * ROWS, other_blk * ROWS - ROWS) + sub

    def column(row):
        return jnp.broadcast_to(row, (128, ROWS)).T

    def cols_of(zo, k, part):
        first = (zo * 4 + yl * 2 + k) * ROWS + part * 128
        return first + lax.broadcasted_iota(jnp.int32, (2 * ROWS, 128), 1)

    def scores(zo, k):
        lanes = pl.ds(pl.multiple_of(k * ROWS, ROWS), ROWS)
        s = lax.dot_general(
            ub_r[...].reshape(2 * ROWS, PROJ), ub_all[zo, lanes, :],
            (((1,), (1,)), ((), ())), preferred_element_type=F32,
        )
        den, pos = den_s[...], pos_s[...]
        for part in (0, 1):
            sp = s[:, part * 128 : (part + 1) * 128]
            cols = cols_of(zo, k, part)
            e = jnp.where(cols == own_row, 0.0, jnp.exp2(sp * (INV_TEMP * LOG2E)))
            e_all[zo, :, pl.ds(pl.multiple_of(k * ROWS + part * 128, 128), 128)] = e
            den += e
            pos += jnp.where(cols == pcol_s[...], sp, 0.0)
        den_s[...] = den
        pos_s[...] = pos

    def other_z(k):
        fy_copy(k).wait_recv()
        part = jnp.dot(feat_o[:, kcut(k)], w_ref[kcut(k), :], preferred_element_type=F32)
        if k == 0:
            u_s[ROWS:] = part
        else:
            u_s[ROWS:] += part

    for s in (1, 2, 3):
        for p in range(4):
            for dr in (0, 1):
                z_arrived(dr, s - 1, p).wait_recv()
                if s < 3 or p // 2 == dr:
                    go(z_copy(dr, s, p))
                if p == 3:
                    go(c_copy(dr, s))
            if s == 1:
                if p == 1:
                    f_t[:, :ROWS] = feat_ref[:, pl.ds(mine, half)].T
                if p == 2:
                    xcp.wait_recv()
                    f_t[:, 2 * ROWS : 3 * ROWS] = f_sib[0].T
                if p == 3:
                    yub.wait_recv()
                    ypairs.wait_recv()
                    pcol_s[:ROWS] = column(pairs_ref[...])
                    pcol_s[ROWS:] = column(pairs_o[...])
                    scores(z, c)
                    c_arrived(0, 0).wait_recv()
                    scores(z, 1 - c)
            else:
                dr = p % 2
                if p >= 2:
                    c_arrived(dr, s - 1).wait_recv()
                scores(origin(dr, s - 1), c if p < 2 else 1 - c)
    for dr in (0, 1):
        scores(origin(dr, 3), c)
    other_z(0)
    for dr in (0, 1):
        c_arrived(dr, 3).wait_recv()
        scores(origin(dr, 3), 1 - c)
    far = origin(0, 4)
    for dr in (0, 1):
        for p in (2 * dr, 2 * dr + 1):
            z_arrived(dr, 3, p).wait_recv()
        go(c_copy(dr, 4))
    scores(far, c)
    for dr in (0, 1):
        c_arrived(dr, 4).wait_recv()
    scores(far, 1 - c)

    sums = jnp.sum(den_s[...].T, axis=0, keepdims=True)
    den_mine[0] = sums[:, :ROWS]
    den_mine[1] = sums[:, ROWS:]
    den_all[0, z * 2 + c] = sums[:, :ROWS]

    def d_copy(dz_, dy, dc):
        to_blk = lax.rem(z + dz_, NZ) * 4 + lax.rem(yl + dy, 2) * 2 + lax.rem(c + dc, 2)
        i = dz_ * 4 + dy * 2 + dc
        return copy(
            den_mine.at[dy], den_all.at[dy, z * 2 + c], d_send.at[i], d_recv.at[i], (to_blk, grp)
        )

    def d_arrived(dz_, dy, dc):
        i = dz_ * 4 + dy * 2 + dc
        ref = den_all.at[dy, lax.rem(z + NZ - dz_, NZ) * 2 + lax.rem(c + dc, 2)]
        return copy(ref, ref, d_send.at[i], d_recv.at[i], (blk, grp))

    docp = copy(den_mine.at[0], den_o, y_send.at[2], y_recv.at[2], ynb)
    for dz_ in (4, 3, 5, 2, 6, 1, 7, 0):
        if dz_ == 2:
            go(docp)
            go(d_copy(0, 1, 0))
        for dy in (0, 1):
            for dc in (0, 1):
                if dz_ or dc:
                    go(d_copy(dz_, dy, dc))

    psum = jnp.sum(pos_s[...].T, axis=0, keepdims=True)
    pos_y[...] = psum[:1, ROWS:]
    pcp = copy(pos_y, pos_x, y_send.at[3], y_recv.at[3], ynb)
    go(pcp)
    pos_ref[...] = psum[:1, :ROWS]
    other_z(1)
    other_z(2)

    def other_half(q):
        cols = pl.ds(pl.multiple_of(c * half + q * cut, cut), cut)
        f_t[q * cut : (q + 1) * cut, ROWS : 2 * ROWS] = feat_o[:, cols].T

    def other_rest():
        other_z(3)
        for q in (0, 1):
            go(fc_copy(q))
        zo_ = u_s[ROWS:]
        inv_o = lax.rsqrt(jnp.sum(zo_ * zo_, axis=1, keepdims=True) + 1e-06)
        u_s[ROWS:] = zo_ * inv_o
        inv_s[ROWS:] = inv_o

    def other_from_sib(q):
        fc_copy(q).wait_recv()
        f_t[q * cut : (q + 1) * cut, 3 * ROWS :] = f_sib[1, :, q * cut : (q + 1) * cut].T

    docp.wait_recv()
    d_arrived(0, 1, 0).wait_recv()
    me2 = z * 2 + c
    den_own = den_all[0, me2] + den_all[1, me2]
    lse_ref[...] = jnp.log(den_own)
    r_s[:ROWS] = column(1.0 / den_own)
    r_s[ROWS:] = column(1.0 / (den_o[...] + den_mine[1]))
    for n, dz_ in enumerate((0, 1, 7, 2, 6, 3, 5, 4)):
        for dy in (0, 1):
            for dc in (0, 1):
                if dz_ or dc:
                    d_arrived(dz_, dy, dc).wait_recv()
        zo = lax.rem(z + NZ - dz_, NZ)
        parts = []
        for k in range(2):
            r_cols = 1.0 / (den_all[0, zo * 2 + k] + den_all[1, zo * 2 + k])
            for part in (0, 1):
                lanes = slice(part * 128, (part + 1) * 128)
                e = e_all[zo, :, k * ROWS + part * 128 : k * ROWS + (part + 1) * 128]
                h = e * (r_s[...] + r_cols[:, lanes])
                h -= jnp.where(cols_of(zo, k, part) == pcol_s[...], 2.0, 0.0)
                parts.append(h.astype(BF16))
        g = jnp.dot(
            jnp.concatenate(parts, axis=1), ub_all[zo], preferred_element_type=F32
        )
        if n == 0:
            acc_s[...] = g
            other_rest()
        else:
            acc_s[...] += g
        if n in (1, 2):
            other_half(n - 1)
        if n in (4, 5):
            other_from_sib(n - 4)

    slope = acc_s[...] * INV_TEMP
    u = u_s[...]
    dz = inv_s[...] * (slope - u * jnp.sum(u * slope, axis=1, keepdims=True))
    dz_ref[...] = dz[:ROWS]
    hi = dz.astype(BF16)
    lo = (dz - hi.astype(F32)).astype(BF16)
    dzh[:2] = hi.reshape(2, ROWS, PROJ)
    xcp = copy(dzh.at[pl.ds(0, 2)], dzh.at[pl.ds(2, 2)], x_send.at[1], x_recv.at[1], sib)
    go(xcp)
    dzl[:2] = lo.reshape(2, ROWS, PROJ)
    lcp = copy(dzl.at[pl.ds(0, 2)], dzl.at[pl.ds(2, 2)], x_send.at[2], x_recv.at[2], sib)

    for t in range(4):
        ft = f_t[t * 256 : (t + 1) * 256, : 2 * ROWS]
        part = jnp.dot(ft, hi, preferred_element_type=F32)
        part += jnp.dot(ft, lo, preferred_element_type=F32)
        pf[t] = part.reshape(4, 64, PROJ)
        if t == 2:
            go(lcp)
    xcp.wait_recv()
    pl.semaphore_wait(in_sem, 4)
    ycp = copy(dzh.at[1], dzx, y_send.at[4], y_recv.at[4], ynb)

    def along(t, first, d):
        if (t % 2 == 0) == first:
            return dev(z, y, c, lax.rem(x + d, 4))
        return dev(z, lax.rem(y + d, 4), c, x)

    def place(t, first):
        return x if (t % 2 == 0) == first else y

    def s1_copy(t, d):
        j = lax.rem(place(t, True) + d, 4)
        return copy(sb1.at[t, j], r1.at[t, d - 1], s1_send.at[t, d - 1], s1_recv.at[t, d - 1], along(t, True, d))

    def s2_copy(t, d):
        j = lax.rem(place(t, False) + d, 4)
        return copy(qf.at[t, j], r2.at[t, d - 1], s2_send.at[t, d - 1], s2_recv.at[t, d - 1], along(t, False, d))

    def out_rows(t, a, b, n):
        start = c * (HID // 2) + t * 256 + a * 64 + b * 16
        return pl.ds(pl.multiple_of(start, 16), n)

    def zcols(j):
        return pl.ds(pl.multiple_of(lax.rem(j, 2) * 256, 256), 256)

    def zpeer(d):
        return dev(lax.rem(z + d, NZ), y, c, x)

    def s3_copy(d):
        j = lax.rem(z + d, NZ)
        return copy(zb.at[j // 2, :, zcols(j)], r3.at[d - 1], s3_send.at[d - 1], s3_recv.at[d - 1], zpeer(d))

    def zrows(j):
        t = j // 2
        odd = lax.rem(t, 2)
        return out_rows(t, x + odd * (y - x), y + odd * (x - y), 16)

    def g3_copy(d, mine_=True):
        j = z if mine_ else lax.rem(z + NZ - d, NZ)
        ref = head_ref.at[zrows(j), zcols(j)]
        return copy(ref, ref, g3_send.at[d - 1], g3_recv.at[d - 1], zpeer(d))

    def g2_copy(t, d, mine_=True):
        b = place(t, False)
        ref = head_ref.at[out_rows(t, place(t, True), b if mine_ else lax.rem(b + 4 - d, 4), 16), :]
        return copy(ref, ref, g2_send.at[t, d - 1], g2_recv.at[t, d - 1], along(t, False, d))

    def g1_copy(t, d, mine_=True):
        a = place(t, True)
        ref = head_ref.at[out_rows(t, a if mine_ else lax.rem(a + 4 - d, 4), 0, 64), :]
        return copy(ref, ref, g1_send.at[t, d - 1], g1_recv.at[t, d - 1], along(t, True, d))

    def gc_copy(t, d):
        a = place(t, True)
        ref = head_ref.at[out_rows(t, lax.rem(a + 4 - d, 4), 0, 64), :]
        return copy(ref, ref, gc_send.at[t, d], gc_recv.at[t, d], sib)

    def gc_arrived(t, d):
        start = (1 - c) * (HID // 2) + t * 256 + lax.rem(place(t, True) + 4 - d, 4) * 64
        ref = head_ref.at[pl.ds(pl.multiple_of(start, 64), 64), :]
        return copy(ref, ref, gc_send.at[t, d], gc_recv.at[t, d], sib)

    D3, D7 = (2, 1, 3), (4, 3, 5, 2, 6, 1, 7)

    def stage1(t):
        ft = f_t[t * 256 : (t + 1) * 256, 2 * ROWS :]
        part = pf[t].reshape(256, PROJ)
        for low in (False, True):
            if low and t == 2:
                lcp.wait_recv()
            if low and t < 2:
                continue
            d = (dzl if low else dzh)[2:].reshape(2 * ROWS, PROJ)
            part = part + jnp.dot(ft, d, preferred_element_type=F32)
        pf[t] = part.reshape(4, 64, PROJ)
        sb1[t] = part.astype(BF16).reshape(4, 64, PROJ)
        for d in D3:
            go(s1_copy(t, d))

    def stage2(t):
        for d in D3:
            s1_copy(t, d).wait_recv()
        total = pf[t, place(t, True)]
        for d in range(3):
            total = total + r1[t, d].astype(F32)
        qf[t] = total.reshape(4, 16, PROJ)
        for d in D3:
            go(s2_copy(t, d))

    def stage3():
        for t in range(4):
            for d in D3:
                s2_copy(t, d).wait_recv()
            zb[t] = qf[t, place(t, False)] + r2[t, 0] + r2[t, 1] + r2[t, 2]
        for d in D7:
            go(s3_copy(d))

    def stage4():
        total = zb[z // 2, :, zcols(z)]
        for d in D7:
            s3_copy(d).wait_recv()
        for d in range(7):
            total = total + r3[d]
        head_ref[zrows(z), zcols(z)] = total.astype(BF16)
        for d in D7:
            go(g3_copy(d))

    def stage5():
        for d in D7:
            g3_copy(d, False).wait_recv()
        for t in range(4):
            for d in D3:
                go(g2_copy(t, d))

    def stage6(t):
        for d in D3:
            g2_copy(t, d, False).wait_recv()
        for d in D3:
            go(g1_copy(t, d))
        go(gc_copy(t, 0))

    def stage7(t):
        for d in D3:
            g1_copy(t, d, False).wait_recv()
            go(gc_copy(t, d))

    for t in range(4):
        stage1(t)
    for t in range(4):
        stage2(t)
    stage3()
    go(ycp)
    flush()
    stage4()
    stage5()
    flush()
    for t in range(4):
        stage6(t)
    ycp.wait_recv()
    dz_ref[...] += dzx[...].astype(F32)
    pcp.wait_recv()
    pos_ref[...] = (pos_ref[...] + pos_x[...]) * INV_TEMP
    for t in range(4):
        stage7(t)
    for t in range(4):
        for d in range(4):
            gc_arrived(t, d).wait_recv()
    flush()


def finish(pos_in, lse_in, dz_in, head_in, pos_ref, lse_ref, dz_ref, head_ref, buf, sem):
    copies = [
        pltpu.make_async_copy(dz_in, dz_ref, sem.at[0]),
        pltpu.make_async_copy(pos_in, pos_ref, sem.at[1]),
        pltpu.make_async_copy(lse_in, lse_ref, sem.at[2]),
    ]
    for cp in copies:
        cp.start()
    for i in range(8):
        rows = slice(i * 256, (i + 1) * 256)
        buf[rows, :] = head_in[rows, :].astype(F32)
        cp = pltpu.make_async_copy(buf.at[rows, :], head_ref.at[rows, :], sem.at[3 + i])
        cp.start()
        copies.append(cp)
    for cp in copies:
        cp.wait()


def on_device(features, head_weight, pairs):
    vmem = pl.BlockSpec(memory_space=pltpu.VMEM)
    dma = pltpu.SemaphoreType.DMA
    pos, lse, dz, head = pl.pallas_call(
        kernel,
        out_shape=(
            pltpu.VMEM((1, ROWS), F32),
            pltpu.VMEM((1, ROWS), F32),
            pltpu.VMEM((ROWS, PROJ), F32),
            pltpu.VMEM((HID, PROJ), BF16),
        ),
        in_specs=[pl.BlockSpec(memory_space=pltpu.HBM)] * 3,
        out_specs=(vmem,) * 4,
        scratch_shapes=[
            pltpu.VMEM((ROWS, HID), BF16),
            pltpu.VMEM((HID, PROJ), BF16),
            pltpu.VMEM((1, ROWS), jnp.int32),
            dma((2 * KCUTS + 1,)),
            pltpu.VMEM((NZ, 2 * ROWS, PROJ), BF16),
            pltpu.VMEM((2, ROWS, PROJ), BF16),
            pltpu.VMEM((NZ, 2 * ROWS, 2 * ROWS), F32),
            pltpu.VMEM((2 * ROWS, PROJ), F32),
            pltpu.VMEM((2 * ROWS, 1), F32),
            pltpu.VMEM((2 * ROWS, 128), jnp.int32),
            pltpu.VMEM((2 * ROWS, 128), F32),
            pltpu.VMEM((2 * ROWS, 128), F32),
            pltpu.VMEM((2 * ROWS, 128), F32),
            pltpu.VMEM((2, 1, ROWS), F32),
            pltpu.VMEM((2, 2 * NZ, 1, ROWS), F32),
            pltpu.VMEM((1, ROWS), F32),
            pltpu.VMEM((1, ROWS), F32),
            pltpu.VMEM((1, ROWS), F32),
            pltpu.VMEM((2 * ROWS, PROJ), F32),
            pltpu.VMEM((ROWS, HID), BF16),
            pltpu.VMEM((1, ROWS), jnp.int32),
            pltpu.VMEM((2, ROWS, HID // 2), BF16),
            pltpu.VMEM((HID // 2, 4 * ROWS), BF16),
            pltpu.VMEM((4, ROWS, PROJ), BF16),
            pltpu.VMEM((4, ROWS, PROJ), BF16),
            pltpu.VMEM((ROWS, PROJ), BF16),
            pltpu.VMEM((4, 4, 64, PROJ), F32),
            pltpu.VMEM((4, 4, 64, PROJ), BF16),
            pltpu.VMEM((4, 3, 64, PROJ), BF16),
            pltpu.VMEM((4, 4, 16, PROJ), F32),
            pltpu.VMEM((4, 3, 16, PROJ), F32),
            pltpu.VMEM((4, 16, PROJ), F32),
            pltpu.VMEM((7, 16, 256), F32),
            pltpu.SemaphoreType.REGULAR,
            dma((2, 4, 4)), dma((2, 4, 4)),
            dma((5,)), dma((5,)),
            dma((KCUTS,)), dma((KCUTS,)),
            dma((2, 5)), dma((2, 5)),
            dma((2,)), dma((2,)),
            dma((32,)), dma((32,)),
            dma((3,)), dma((3,)),
            dma((4, 3)), dma((4, 3)),
            dma((4, 3)), dma((4, 3)),
            dma((7,)), dma((7,)),
            dma((7,)), dma((7,)),
            dma((4, 3)), dma((4, 3)),
            dma((4, 3)), dma((4, 3)),
            dma((4, 4)), dma((4, 4)),
        ],
        compiler_params=pltpu.CompilerParams(
            collective_id=0, has_side_effects=True, vmem_limit_bytes=44 << 20
        ),
        name="ntxent",
    )(*[pltpu.with_memory_space_constraint(a, pltpu.HBM) for a in (features[0], head_weight, pairs)])
    inputs = [pltpu.with_memory_space_constraint(a, pltpu.VMEM) for a in (pos, lse, dz, head)]
    pos, lse, dz, head = pl.pallas_call(
        finish,
        out_shape=(
            jax.ShapeDtypeStruct((1, ROWS), F32),
            jax.ShapeDtypeStruct((1, ROWS), F32),
            jax.ShapeDtypeStruct((ROWS, PROJ), F32),
            jax.ShapeDtypeStruct((HID, PROJ), F32),
        ),
        in_specs=[vmem] * 4,
        out_specs=(pl.BlockSpec(memory_space=pl.ANY),) * 4,
        scratch_shapes=[pltpu.VMEM((HID, PROJ), F32), dma((11,))],
        compiler_params=pltpu.CompilerParams(vmem_limit_bytes=16 << 20),
        name="finish",
    )(*inputs)
    return pos, lse, dz[None], head


def solution(mesh):
    in_specs = (P("group", "blk", None), P(), P("group", "blk"))
    out_specs = (P("group", "blk"), P("group", "blk"), P("group", "blk", None), P())
    return jax.shard_map(
        on_device, mesh=mesh, in_specs=in_specs, out_specs=out_specs, check_vma=False
    )
```
